128 devices in a mesh: row: 4 (over y), col: 4 (over x_lo, core), freq: 8 (over z, x_hi).
Axes of the slice: x: 4 (x_hi: 2, x_lo: 2; x = x_hi * 2 + x_lo), y: 4, z: 4, core: 2. Of those that a mesh axis runs over, the one named last changes fastest.
Arguments:
- traces: bfloat16 [1280, 224, 512], P(('row', 'col'), 'freq'), may hold values from -6 to 6
- window_mask: int32 [1280, 224], P(('row', 'col'), 'freq'), may hold values 0 or 1
Outputs:
- cross_spectra: bfloat16 [2, 256, 1280, 1280], P(None, 'freq', 'row', 'col')
The draws below stay inside these ranges and needn't reach their ends.
All inputs are finite; a program needn't handle non-finite values. No bound on the sum of `window_mask` on one device may be relied on, other than what follows from the above.
Results may differ from the reference program's by a relative error of at most 0.0065.
Values may be sent and summed in bfloat16 or wider, within the bound.
A program may use at most 192 MiB of HBM per device.

```python
import math
import jax
import jax.numpy as jnp
from jax import lax

SAMPLES = 512
BINS = 256
STATIONS = 1280
WINDOWS = 224


def touch_ends(drawn, rng, least, top_value):
    longest = drawn.shape.index(max(drawn.shape))
    spots = []
    for shift in (0, 1):
        where = [jax.random.randint(jax.random.fold_in(rng, axis), (), 0, length) for axis, length in enumerate(drawn.shape)]
        where[longest] = (where[longest] + shift) % drawn.shape[longest]
        spots.append(tuple(where))
    return drawn.at[spots[0]].set(least).at[spots[1]].set(top_value)


def levels(stream_key, extent, cuts, low, top_value):
    gain, own = 1.0, jax.random.fold_in(stream_key, 6)
    for position, blocks in cuts:
        steps = jnp.exp(jax.random.uniform(jax.random.fold_in(own, position), (blocks,), jnp.float32, low / len(cuts), top_value / len(cuts)))
        gain = gain * jnp.repeat(steps, extent[position] // blocks).reshape([-1 if axis == position else 1 for axis in range(len(extent))])
    return gain


def normal_values(rng, dims, scale, reach, pieces=(), kind=jnp.bfloat16):
    entries = scale * jax.random.normal(rng, dims, jnp.float32)
    if pieces:
        entries = entries * levels(rng, dims, pieces, -0.22, 0.18)
    return jnp.clip(entries, -reach, reach).astype(kind)


def setup_inputs(seed: int = 0) -> dict:
    key_of = jax.random.split(jax.random.key(seed), 3)
    return {
        "traces": normal_values(key_of[0], (STATIONS, WINDOWS, SAMPLES), 1.0, 6.0, ((0, 16), (1, 8))),
        "window_mask": touch_ends((jax.random.randint(key_of[1], (STATIONS, WINDOWS), 0, 4) < 3).astype(jnp.int32), jax.random.fold_in(key_of[1], 1), 0, 1),
    }


epsilon = 1e-06

def dft_table():
    sample_idx = jnp.arange(SAMPLES, dtype=jnp.int32)
    bin_idx = jnp.arange(BINS, dtype=jnp.int32)
    phase = bin_idx[:, None] * sample_idx[None, :] % SAMPLES
    angles = 2.0 * math.pi / SAMPLES * phase.astype(jnp.float32)
    taper = 0.5 - 0.5 * jnp.cos(2.0 * math.pi / SAMPLES * sample_idx.astype(jnp.float32))
    stacked = jnp.stack([taper[None, :] * jnp.cos(angles), -taper[None, :] * jnp.sin(angles)], axis=1)
    return stacked.reshape(2 * BINS, SAMPLES).astype(jnp.bfloat16)

def reference(traces, window_mask):
    dft = dft_table()
    flat = traces.reshape(STATIONS * WINDOWS, SAMPLES)
    spectrum = jnp.dot(flat, dft.T, preferred_element_type=jnp.float32).reshape(STATIONS, WINDOWS, 2 * BINS)
    energy = lax.optimization_barrier(jnp.mean(spectrum * spectrum, axis=2))
    factor = window_mask.astype(jnp.float32) * lax.rsqrt(energy + epsilon)
    whitened = (spectrum * factor[:, :, None]).astype(jnp.bfloat16)
    by_bin = jnp.transpose(whitened.reshape(STATIONS, WINDOWS, BINS, 2), (2, 3, 0, 1))
    norm_scale = 1.0 / math.sqrt(WINDOWS)

    def one_bin(planes):
        real_plane = planes[0]
        imag_plane = planes[1]
        real_real = jnp.dot(real_plane, real_plane.T, preferred_element_type=jnp.float32)
        imag_imag = jnp.dot(imag_plane, imag_plane.T, preferred_element_type=jnp.float32)
        imag_real = jnp.dot(imag_plane, real_plane.T, preferred_element_type=jnp.float32)
        real_imag = jnp.dot(real_plane, imag_plane.T, preferred_element_type=jnp.float32)
        both = jnp.stack([(real_real + imag_imag) * norm_scale, (imag_real - real_imag) * norm_scale])
        return both.astype(jnp.bfloat16)
    result = lax.map(one_bin, by_bin)
    return jnp.transpose(result, (1, 0, 2, 3))
```

```python
import math

import jax
import jax.numpy as jnp
import numpy as np
from jax import lax
from jax.experimental import pallas as pl
from jax.experimental.pallas import tpu as pltpu
from jax.sharding import PartitionSpec as P

SAMPLES = 512
BINS = 256
EPSILON = 1e-06
NS = 80
NW = 28
PW = 32
NT = 16
LANES = 128
WINDOWS = 224
MESH = pl.DeviceIdType.MESH
NT_DIMS = (((1,), (1,)), ((), ()))


def dft_table():
    t = np.arange(SAMPLES, dtype=np.int64)
    k = np.arange(BINS, dtype=np.int64)
    angles = 2.0 * math.pi / SAMPLES * ((k[:, None] * t[None, :]) % SAMPLES)
    taper = 0.5 - 0.5 * np.cos(2.0 * math.pi / SAMPLES * t)
    stacked = np.stack([taper * np.cos(angles), -taper * np.sin(angles)], axis=1)
    return stacked.reshape(2 * BINS, SAMPLES).astype(np.float32)


def spectra_kernel(dft_ref, traces_ref, mask_ref, out_ref, rows):
    def one_window(w, carry):
        y = lax.dot_general(
            dft_ref[...], traces_ref[w], NT_DIMS, preferred_element_type=jnp.float32
        )
        energy = jnp.sum(y * y, axis=0, keepdims=True) * (1.0 / SAMPLES)
        factor = mask_ref[w].astype(jnp.float32) * lax.rsqrt(energy + EPSILON)
        rows[pl.ds(w, 2 * BINS, stride=PW), :] = y * factor
        return carry

    lax.fori_loop(0, NW, one_window, 0)
    for w in range(NW, PW):
        rows[pl.ds(w, 2 * BINS, stride=PW), :] = jnp.zeros((2 * BINS, NS), jnp.float32)
    eye = (
        lax.broadcasted_iota(jnp.int32, (NS, NS), 0)
        == lax.broadcasted_iota(jnp.int32, (NS, NS), 1)
    ).astype(jnp.float32).astype(jnp.bfloat16)

    def one_group(g, carry):
        start = pl.multiple_of(g * 2 * LANES, 2 * LANES)
        block = rows[pl.ds(start, 2 * LANES), :].astype(jnp.bfloat16)
        turned = lax.dot_general(eye, block, NT_DIMS, preferred_element_type=jnp.float32)
        turned = turned.astype(jnp.bfloat16)
        f, pair = g // (NT // 2), g % (NT // 2)
        out_ref[f, 2 * pair] = turned[:, :LANES]
        out_ref[f, 2 * pair + 1] = turned[:, LANES:]
        return carry

    lax.fori_loop(0, 8 * NT // 2, one_group, 0)


def spectra(dft, traces, window_mask):
    return pl.pallas_call(
        spectra_kernel,
        out_shape=jax.ShapeDtypeStruct((8, NT, NS, LANES), jnp.bfloat16),
        in_specs=[pl.BlockSpec(memory_space=pltpu.VMEM)] * 3,
        out_specs=pl.BlockSpec(memory_space=pltpu.VMEM),
        scratch_shapes=[pltpu.VMEM((2 * BINS * PW, NS), jnp.float32)],
        compiler_params=pltpu.CompilerParams(vmem_limit_bytes=32 * 2**20),
        name="spectra",
    )(dft, traces, window_mask)


def exchange_kernel(
    mine, out_ref, buf,
    send_b, send_x, send_y, send_c,
    recv_b, recv_x, recv_o, recv_p, recv_l, recv_r,
):
    y = lax.axis_index("row")
    col = lax.axis_index("col")
    freq = lax.axis_index("freq")
    xl, core = col // 2, col % 2
    z, xh = freq // 2, freq % 2
    pair_y = y + 1 - 2 * (y % 2)
    outer_y = 3 - y
    is_source = (y // 2) == xl
    other_col = col + 1 - 2 * core
    x_col = (1 - xl) * 2 + core

    def dev(row_=None, col_=None, freq_=None):
        return (
            y if row_ is None else row_,
            col if col_ is None else col_,
            freq if freq_ is None else freq_,
        )

    barrier = pltpu.get_barrier_semaphore()
    peers = [dev(freq_=((z + k) % 4) * 2 + xh) for k in (1, 2, 3)]
    peers += [dev(col_=x_col, freq_=((z + k) % 4) * 2 + 1 - xh) for k in range(4)]
    peers += [dev(col_=x_col), dev(row_=pair_y), dev(row_=outer_y), dev(col_=other_col)]
    for peer in peers:
        pl.semaphore_signal(barrier, inc=1, device_id=peer, device_id_type=MESH)
    pl.semaphore_wait(barrier, len(peers))

    def remote(src, dst, send, recv, peer):
        return pltpu.make_async_remote_copy(
            src_ref=src, dst_ref=dst, send_sem=send, recv_sem=recv,
            device_id=peer, device_id_type=MESH,
        )

    def copies_b(t):
        dst = buf.at[t, core, xl, xh, z]
        made = []
        for k in (1, 2, 3):
            f = ((z + k) % 4) * 2 + xh
            made.append(remote(mine.at[f, t], dst, send_b.at[t, k], recv_b.at[t, 0], dev(freq_=f)))
        for k in range(4):
            f = ((z + k) % 4) * 2 + 1 - xh
            made.append(
                remote(mine.at[f, t], dst, send_b.at[t, 4 + k], recv_b.at[t, 1],
                       dev(col_=x_col, freq_=f))
            )
        local = pltpu.make_async_copy(mine.at[freq, t], dst, send_b.at[t, 0])
        return made, local

    def copies_x(t):
        own = buf.at[t, core, xl, xh]
        theirs = buf.at[t, core, 1 - xl, 1 - xh]
        return [
            remote(own, own, send_x.at[t, 0], recv_x.at[t, 0], dev(col_=x_col)),
            remote(theirs, theirs, send_x.at[t, 1], recv_x.at[t, 1], dev(col_=x_col)),
        ]

    def slot_of(row_):
        return jnp.where(row_ == col, 2 + core, 4)

    def copy_to_pair(t):
        src = buf.at[t, jnp.where(is_source, core, slot_of(outer_y))]
        dst = buf.at[t, slot_of(jnp.where(is_source, y, outer_y))]
        return remote(src, dst, send_y.at[t, 0], recv_p.at[t], dev(row_=pair_y))

    def copy_to_outer(t):
        return remote(
            buf.at[t, core], buf.at[t, slot_of(y)], send_y.at[t, 1], recv_o.at[t],
            dev(row_=outer_y),
        )

    def copy_core_l(t):
        half = buf.at[t, core]
        return remote(half, half, send_c.at[t, 0], recv_l.at[t], dev(col_=other_col))

    needs_r = jnp.logical_not(col == y)
    gives_r = jnp.logical_not(other_col == y)

    def copy_core_r(t):
        return remote(
            buf.at[t, 4], buf.at[t, 2 + core], send_c.at[t, 1], recv_r.at[t],
            dev(col_=other_col),
        )

    def start_b(t, carry):
        made, local = copies_b(t)
        for c in made:
            c.start()
        local.start()
        return carry

    lax.fori_loop(0, NT, start_b, 0)

    def wait_only(ref, sem):
        pltpu.make_async_copy(ref, ref, sem).wait()

    r_slot = jnp.where(col == y, 0, 2)
    lane = lax.broadcasted_iota(jnp.int32, (1, LANES), 1)
    even = (lane // PW) % 2 == 0
    first = lane < 2 * PW
    scale = 1.0 / math.sqrt(WINDOWS)

    def rows_of(t, slot, src):
        parts = [buf[t, slot + c % 2, c // 2, src // 4, src % 4] for c in range(4)]
        return jnp.concatenate(parts, axis=0)

    def multiply(t):
        right = jnp.concatenate([rows_of(t, r_slot, src) for src in range(8)], axis=1)
        left = [[], [], [], []]
        zero = jnp.zeros((4 * NS, LANES), jnp.bfloat16)
        for src in range(8):
            tile = rows_of(t, 0, src)
            wide = tile.astype(jnp.float32)
            ahead = pltpu.roll(wide, LANES - PW, 1)
            back = pltpu.roll(wide, PW, 1)
            turned = jnp.where(even, ahead, -back).astype(jnp.bfloat16)
            left[0].append(jnp.where(first, tile, zero))
            left[1].append(jnp.where(first, turned, zero))
            left[2].append(jnp.where(first, zero, tile))
            left[3].append(jnp.where(first, zero, turned))
        for v in range(4):
            lhs = jnp.concatenate(left[v], axis=1)
            product = lax.dot_general(lhs, right, NT_DIMS, preferred_element_type=jnp.float32)
            out_ref[v % 2, 2 * t + v // 2] = (product * scale).astype(jnp.bfloat16)

    def step(tau, carry):
        @pl.when(tau < NT)
        def _():
            t = tau
            _, local = copies_b(t)
            local.wait()
            wait_only(buf.at[t, core, xl, xh, pl.ds(0, 3)], recv_b.at[t, 0])
            wait_only(buf.at[t, core, 1 - xl, 1 - xh], recv_b.at[t, 1])
            for c in copies_x(t):
                c.start()

        @pl.when(jnp.logical_and(tau >= 1, tau < NT + 1))
        def _():
            t = tau - 1
            for c in copies_x(t):
                c.wait_recv()

            @pl.when(is_source)
            def _():
                copy_to_outer(t).start()
                copy_to_pair(t).start()

            copy_core_l(t).start()

        @pl.when(jnp.logical_and(tau >= 2, tau < NT + 2))
        def _():
            t = tau - 2

            @pl.when(jnp.logical_not(is_source))
            def _():
                wait_only(buf.at[t, slot_of(outer_y)], recv_o.at[t])
                copy_to_pair(t).start()

        @pl.when(jnp.logical_and(tau >= 3, tau < NT + 3))
        def _():
            t = tau - 3
            wait_only(buf.at[t, 4], recv_p.at[t])

            @pl.when(gives_r)
            def _():
                copy_core_r(t).start()

        @pl.when(tau >= 4)
        def _():
            t = tau - 4
            copy_core_l(t).wait_recv()

            @pl.when(needs_r)
            def _():
                copy_core_r(t).wait_recv()

            multiply(t)

        return carry

    lax.fori_loop(0, NT + 4, step, 0)

    def finish(t, carry):
        made, _ = copies_b(t)
        for c in made + copies_x(t):
            c.wait_send()
        copy_to_pair(t).wait_send()
        copy_core_l(t).wait_send()

        @pl.when(is_source)
        def _():
            copy_to_outer(t).wait_send()

        @pl.when(gives_r)
        def _():
            copy_core_r(t).wait_send()

        return carry

    lax.fori_loop(0, NT, finish, 0)


def cross(mine):
    dma = pltpu.SemaphoreType.DMA
    return pl.pallas_call(
        exchange_kernel,
        out_shape=jax.ShapeDtypeStruct((2, 32, 320, 320), jnp.bfloat16),
        in_specs=[pl.BlockSpec(memory_space=pl.ANY)],
        out_specs=pl.BlockSpec(memory_space=pltpu.VMEM),
        scratch_shapes=[
            pltpu.VMEM((NT, 5, 2, 2, 4, NS, LANES), jnp.bfloat16),
            dma((NT, 8)), dma((NT, 2)), dma((NT, 2)), dma((NT, 2)),
            dma((NT, 2)), dma((NT, 2)), dma((NT,)), dma((NT,)), dma((NT,)), dma((NT,)),
        ],
        compiler_params=pltpu.CompilerParams(
            collective_id=0, has_side_effects=True, vmem_limit_bytes=60 * 2**20
        ),
        cost_estimate=pl.CostEstimate(
            flops=12 * 10**9, bytes_accessed=20 * 10**6, transcendentals=0
        ),
        name="exchange",
    )(mine)


def shards(traces, window_mask):
    dft = jnp.asarray(dft_table().astype(jnp.bfloat16))
    mask = jnp.transpose(window_mask)[:, None, :]
    mine = spectra(dft, jnp.transpose(traces, (1, 0, 2)), mask)
    return cross(mine)


def solution(mesh):
    placed = (P(("row", "col"), "freq", None), P(("row", "col"), "freq"))
    return jax.shard_map(
        shards, mesh=mesh, in_specs=placed, out_specs=P(None, "freq", "row", "col"), check_vma=False
    )
```

```python
import math

import jax
import jax.numpy as jnp
import numpy as np
from jax import lax
from jax.experimental import pallas as pl
from jax.experimental.pallas import tpu as pltpu
from jax.sharding import PartitionSpec as P

SAMPLES = 512
BINS = 256
EPSILON = 1e-06
NS = 80
NW = 28
LANES = 128
NT = 14
PERIOD = 7
CHUNKS = 4
WINDOWS = 224
MESH = pl.DeviceIdType.MESH
NT_DIMS = (((1,), (1,)), ((), ()))

L1, L2, L3, L4, L5, L6 = 1, 2, 4, 6, 8, 9


def dft_table():
    t = np.arange(SAMPLES, dtype=np.int64)
    k = np.arange(BINS, dtype=np.int64)
    angles = 2.0 * math.pi / SAMPLES * ((k[:, None] * t[None, :]) % SAMPLES)
    taper = 0.5 - 0.5 * np.cos(2.0 * math.pi / SAMPLES * t)
    stacked = np.stack([taper * np.cos(angles), -taper * np.sin(angles)], axis=1)
    return stacked.reshape(2 * BINS, SAMPLES).astype(np.float32)


def kernel(
    dft_hbm, traces_hbm, mask_ref, out_ref,
    mine, wbuf, buf, in_sem, sends, recvs,
):
    y = lax.axis_index("row")
    col = lax.axis_index("col")
    freq = lax.axis_index("freq")
    xl, core = col // 2, col % 2
    z, xh = freq // 2, freq % 2
    pair_y = y + 1 - 2 * (y % 2)
    outer_y = 3 - y
    far_y = 3 - pair_y
    is_source = (y // 2) == xl
    is_relay = jnp.logical_not(is_source)
    other_col = col + 1 - 2 * core
    x_col = (1 - xl) * 2 + core
    x_freq = z * 2 + 1 - xh

    others = [((z + k) % 4) for k in (1, 3, 2)]
    z_devs = [(y, col, o * 2 + xh) for o in others]
    twin = (y, x_col, freq)
    cross = (y, x_col, x_freq)
    pair = (pair_y, col, freq)
    outer = (outer_y, col, freq)
    mate = (y, other_col, freq)

    barrier = pltpu.get_barrier_semaphore()
    peers = z_devs + [twin, cross, pair, outer, mate]
    for peer in peers:
        pl.semaphore_signal(barrier, inc=1, device_id=peer, device_id_type=MESH)

    def remote(src, dst, send, recv, peer):
        return pltpu.make_async_remote_copy(
            src_ref=src, dst_ref=dst, send_sem=send, recv_sem=recv,
            device_id=peer, device_id_type=MESH,
        )

    def slot_of(row_, col_=col):
        return jnp.where(row_ == col_, 2 + core, 4)

    def free(t, row_, i):
        return buf.at[t, jnp.where(row_ == col, 2, 4), 0, i]

    def z_copies(t):
        made = []
        for k in range(3):
            made.append(remote(mine.at[t, others[k] * 2 + xh], buf.at[t, core, xl, xh, z],
                               sends.at[t, 2 * k], recvs.at[t, 0], z_devs[k]))
            made.append(remote(mine.at[t, others[k] * 2 + 1 - xh], wbuf.at[t, z],
                               sends.at[t, 2 * k + 1], recvs.at[t, 1], z_devs[k]))
        return made

    def own_copies(t):
        return [
            pltpu.make_async_copy(mine.at[t, freq], buf.at[t, core, xl, xh, z], sends.at[t, 6]),
            pltpu.make_async_copy(mine.at[t, x_freq], wbuf.at[t, z], sends.at[t, 7]),
        ]

    def same(t, place, send, recv, peer):
        ref = buf.at[(t,) + place]
        return remote(ref, ref, sends.at[t, send], recvs.at[t, recv], peer)

    def to_cross(t):
        return remote(wbuf.at[t], buf.at[t, core, xl, xh], sends.at[t, 8], recvs.at[t, 2], cross)

    def to_twin_a(t):
        return same(t, (core, xl, xh), 9, 3, twin)

    def to_twin_b(t):
        return same(t, (core, 1 - xl, 1 - xh), 10, 4, twin)

    def core_l(t):
        return same(t, (core,), 11, 5, mate)

    def core_r(t):
        return remote(buf.at[t, 4], buf.at[t, 2 + core], sends.at[t, 12], recvs.at[t, 6], mate)

    def source_pair(t):
        return remote(buf.at[t, core, 1 - xl], buf.at[t, slot_of(y), 1 - xl],
                      sends.at[t, 13], recvs.at[t, 7], pair)

    def source_outer_a(t):
        return remote(buf.at[t, core, xl], buf.at[t, slot_of(y), xl],
                      sends.at[t, 14], recvs.at[t, 8], outer)

    def source_outer_b(t):
        return remote(buf.at[t, core, 1 - xl, xh], buf.at[t, slot_of(y), 1 - xl, xh],
                      sends.at[t, 15], recvs.at[t, 9], outer)

    def source_w_pair(t):
        return remote(free(t, y, 0), free(t, pair_y, 1), sends.at[t, 16], recvs.at[t, 10], pair)

    def source_cross_a(t):
        return remote(free(t, y, 0), buf.at[t, slot_of(outer_y, x_col), xl, xh],
                      sends.at[t, 17], recvs.at[t, 11], cross)

    def source_cross_b(t):
        return remote(free(t, y, 1), buf.at[t, slot_of(far_y, x_col), xl, xh],
                      sends.at[t, 18], recvs.at[t, 12], cross)

    def relay_w_outer(t):
        return remote(wbuf.at[t], free(t, outer_y, 0), sends.at[t, 13], recvs.at[t, 9], outer)

    def relay_pair_a(t):
        return same(t, (slot_of(outer_y), xl), 14, 7, pair)

    def relay_pair_b(t):
        return same(t, (slot_of(outer_y), 1 - xl, xh), 15, 10, pair)

    def relay_outer(t):
        return same(t, (slot_of(far_y), xl), 16, 8, outer)

    needs_r = jnp.logical_not(col == y)
    gives_r = jnp.logical_not(other_col == y)

    def transform(dft_ref, traces_ref, rows):
        per = NW // CHUNKS
        dft_copy = pltpu.make_async_copy(dft_hbm, dft_ref, in_sem.at[CHUNKS])
        dft_copy.start()

        def chunk_copy(i):
            part = pl.ds(i * per, per)
            return pltpu.make_async_copy(traces_hbm.at[part], traces_ref.at[part], in_sem.at[i])

        for i in range(CHUNKS):
            chunk_copy(i).start()

        dft_copy.wait()

        def one_chunk(i, carry):
            chunk_copy(i).wait()
            for j in range(per):
                w = i * per + j
                spectrum = lax.dot_general(
                    dft_ref[...], traces_ref[w], NT_DIMS, preferred_element_type=jnp.float32
                )
                energy = jnp.sum(spectrum * spectrum, axis=0, keepdims=True) * (1.0 / SAMPLES)
                factor = mask_ref[pl.ds(w, 1), :].astype(jnp.float32) * lax.rsqrt(energy + EPSILON)
                rows[pl.ds(w, 2 * BINS, stride=NW), :] = spectrum * factor
            return carry

        lax.fori_loop(0, CHUNKS, one_chunk, 0)

        pl.semaphore_wait(barrier, len(peers))

        def turn(t, carry):
            for f in range(8):
                start = pl.multiple_of((f * NT + t) * LANES, LANES)
                mine[t, f] = rows[pl.ds(start, LANES), :].T.astype(jnp.bfloat16)
            for c in z_copies(t) + own_copies(t):
                c.start()
            return carry

        lax.fori_loop(0, NT, turn, 0)

    pl.run_scoped(
        transform,
        pltpu.VMEM((2 * BINS, SAMPLES), jnp.bfloat16),
        pltpu.VMEM((NW, NS, SAMPLES), jnp.bfloat16),
        pltpu.VMEM((2 * BINS * NW, NS), jnp.float32),
    )

    def wait_only(ref, sem):
        pltpu.make_async_copy(ref, ref, sem).wait()

    r_slot = jnp.where(col == y, 0, 2)
    lane = lax.broadcasted_iota(jnp.int32, (1, LANES), 1)
    scale = 1.0 / math.sqrt(WINDOWS)

    def rows_of(t, slot, src):
        parts = [buf[t, slot + c % 2, c // 2, src // 4, src % 4] for c in range(4)]
        return jnp.concatenate(parts, axis=0)

    def roll(tile, by):
        return pltpu.roll(tile.astype(jnp.float32), by, 1)

    def masked(tile, ahead, back, lo, hi):
        inside = (lane >= lo) & (lane < hi)
        turned = jnp.where(lane < lo + NW, ahead, -back).astype(jnp.bfloat16)
        zero = jnp.zeros_like(tile)
        return jnp.where(inside, tile, zero), jnp.where(inside, turned, zero)

    def main(lhs):
        def put(k, tile, ahead, back, lo, hi):
            plain, turned = masked(tile, ahead, back, lo, hi)
            lhs[pl.ds(0, 4 * NS), pl.ds(k * LANES, LANES)] = plain
            lhs[pl.ds(4 * NS, 4 * NS), pl.ds(k * LANES, LANES)] = turned

        def store(b, rhs):
            product = lax.dot_general(
                lhs[:, pl.ds(0, LANES * len(rhs))], jnp.concatenate(rhs, axis=1), NT_DIMS,
                preferred_element_type=jnp.float32,
            )
            product = (product * scale).astype(jnp.bfloat16)
            out_ref[0, b] = product[: 4 * NS]
            out_ref[1, b] = product[4 * NS :]

        def whole_bin(t, b):
            lo = 2 * NW * b - LANES * t
            for s in range(8):
                tile = rows_of(t, 0, s)
                put(s, tile, roll(tile, LANES - NW), roll(tile, NW), lo, lo + 2 * NW)
            store(b, [rows_of(t, r_slot, s) for s in range(8)])

        def split_bin(t, b):
            lo = 2 * NW * b - LANES * t
            for s in range(8):
                before, tile = rows_of(t - 1, 0, s), rows_of(t, 0, s)
                ahead = roll(tile, LANES - NW)
                back = roll(before, NW)
                put(2 * s, before, jnp.where(lane < LANES - NW, roll(before, LANES - NW), ahead),
                    back, lo + LANES, LANES)
                put(2 * s + 1, tile, ahead, jnp.where(lane < NW, back, roll(tile, NW)),
                    lo, lo + 2 * NW)
            store(b, [rows_of(t - 1 + i, r_slot, s) for s in range(8) for i in range(2)])

        def multiply(t):
            first = (LANES * t) // (2 * NW)
            last = (LANES * (t + 1)) // (2 * NW)
            split = (t % PERIOD != 0).astype(jnp.int32)

            @pl.when(t % PERIOD != 0)
            def _():
                split_bin(t, first)

            def one(b, carry):
                whole_bin(t, b)
                return carry

            lax.fori_loop(first + split, last, one, 0)

        def at(tau, lag):
            return jnp.logical_and(tau >= lag, tau < NT + lag)

        def step(tau, carry):
            @pl.when(tau < NT)
            def _():
                t = tau
                for c in own_copies(t):
                    c.wait()
                wait_only(buf.at[t, core, xl, xh, pl.ds(0, 3)], recvs.at[t, 0])
                wait_only(wbuf.at[t, pl.ds(0, 3)], recvs.at[t, 1])
                to_cross(t).start()
                to_twin_a(t).start()

                @pl.when(is_relay)
                def _():
                    relay_w_outer(t).start()

            @pl.when(at(tau, L1))
            def _():
                t = tau - L1
                to_cross(t).wait_recv()
                to_twin_b(t).start()

            @pl.when(at(tau, L2))
            def _():
                t = tau - L2
                to_twin_a(t).wait_recv()
                to_twin_b(t).wait_recv()

                @pl.when(is_source)
                def _():
                    source_outer_a(t).start()
                    source_outer_b(t).start()
                    source_pair(t).start()

                core_l(t).start()

            @pl.when(at(tau, L3))
            def _():
                t = tau - L3

                @pl.when(is_relay)
                def _():
                    source_outer_a(t).wait_recv()
                    relay_pair_a(t).start()
                    source_outer_b(t).wait_recv()
                    relay_pair_b(t).start()

                @pl.when(is_source)
                def _():
                    relay_w_outer(t).wait_recv()
                    source_w_pair(t).start()
                    source_cross_a(t).start()

            @pl.when(at(tau, L4))
            def _():
                t = tau - L4

                @pl.when(is_relay)
                def _():
                    relay_pair_a(t).wait_recv()
                    relay_outer(t).start()
                    relay_pair_b(t).wait_recv()

                @pl.when(is_source)
                def _():
                    source_w_pair(t).wait_recv()
                    source_cross_b(t).start()

            @pl.when(at(tau, L5))
            def _():
                t = tau - L5

                @pl.when(is_relay)
                def _():
                    source_cross_a(t).wait_recv()
                    source_cross_b(t).wait_recv()

                @pl.when(is_source)
                def _():
                    source_pair(t).wait_recv()
                    relay_outer(t).wait_recv()

                @pl.when(gives_r)
                def _():
                    core_r(t).start()

            @pl.when(tau >= L6)
            def _():
                t = tau - L6
                core_l(t).wait_recv()

                @pl.when(needs_r)
                def _():
                    core_r(t).wait_recv()

                multiply(t)

            return carry

        lax.fori_loop(0, NT + L6, step, 0)

    pl.run_scoped(main, pltpu.VMEM((8 * NS, 16 * LANES), jnp.bfloat16))

    def finish(t, carry):
        for c in z_copies(t) + [to_cross(t), to_twin_a(t), to_twin_b(t), core_l(t)]:
            c.wait_send()

        @pl.when(is_source)
        def _():
            for c in (source_pair, source_outer_a, source_outer_b, source_w_pair,
                      source_cross_a, source_cross_b):
                c(t).wait_send()

        @pl.when(is_relay)
        def _():
            for c in (relay_w_outer, relay_pair_a, relay_pair_b, relay_outer):
                c(t).wait_send()

        @pl.when(gives_r)
        def _():
            core_r(t).wait_send()

        return carry

    lax.fori_loop(0, NT, finish, 0)


def shards(traces, window_mask):
    dft = jnp.asarray(dft_table().astype(jnp.bfloat16))
    dma = pltpu.SemaphoreType.DMA
    bf16 = jnp.bfloat16
    return pl.pallas_call(
        kernel,
        out_shape=jax.ShapeDtypeStruct((2, 32, 320, 320), bf16),
        in_specs=[
            pl.BlockSpec(memory_space=pl.ANY),
            pl.BlockSpec(memory_space=pl.ANY),
            pl.BlockSpec(memory_space=pltpu.VMEM),
        ],
        out_specs=pl.BlockSpec(memory_space=pltpu.VMEM),
        scratch_shapes=[
            pltpu.VMEM((NT, 8, NS, LANES), bf16),
            pltpu.VMEM((NT, 4, NS, LANES), bf16),
            pltpu.VMEM((NT, 5, 2, 2, 4, NS, LANES), bf16),
            dma((CHUNKS + 1,)), dma((NT, 19)), dma((NT, 13)),
        ],
        compiler_params=pltpu.CompilerParams(
            collective_id=0, has_side_effects=True, vmem_limit_bytes=36 * 2**20
        ),
        cost_estimate=pl.CostEstimate(
            flops=12 * 10**9, bytes_accessed=20 * 10**6, transcendentals=0
        ),
        name="cross_spectra",
    )(dft, jnp.transpose(traces, (1, 0, 2)), jnp.transpose(window_mask))


def solution(mesh):
    placed = (P(("row", "col"), "freq", None), P(("row", "col"), "freq"))
    return jax.shard_map(
        shards, mesh=mesh, in_specs=placed, out_specs=P(None, "freq", "row", "col"), check_vma=False
    )
```

```python
import math

import jax
import jax.numpy as jnp
import numpy as np
from jax import lax
from jax.experimental import pallas as pl
from jax.experimental.pallas import tpu as pltpu
from jax.sharding import PartitionSpec as P

SAMPLES = 512
BINS = 256
EPSILON = 1e-06
NS = 80
NW = 28
LANES = 128
NT = 14
PERIOD = 7
CHUNKS = 2
WINDOWS = 224
MESH = pl.DeviceIdType.MESH
NT_DIMS = (((1,), (1,)), ((), ()))

ORDER = (
    ("own", 0), ("turn", -3), ("loop_b", 5), ("relay_a", 1), ("twin_b", 1), ("send_a", 2),
    ("loop_a", 3), ("relay_b", 3), ("multiply", 7), ("send_b", 2), ("relay_c", 3), ("rows", 5),
)
Z, X1, CA, CB, CL, CR, O4, O1, O2, P4, P1, P2, XW = range(13)


def dft_table():
    t = np.arange(SAMPLES, dtype=np.int64)
    k = np.arange(BINS, dtype=np.int64)
    angles = 2.0 * math.pi / SAMPLES * ((k[:, None] * t[None, :]) % SAMPLES)
    taper = 0.5 - 0.5 * np.cos(2.0 * math.pi / SAMPLES * t)
    stacked = np.stack([taper * np.cos(angles), -taper * np.sin(angles)], axis=1)
    return stacked.reshape(2 * BINS, SAMPLES).astype(np.float32)


def kernel(
    dft_ref, traces_ref, mask_ref, out_ref, mine, wbuf, buf, sends, recvs,
):
    y = lax.axis_index("row")
    col = lax.axis_index("col")
    freq = lax.axis_index("freq")
    xl, core = col // 2, col % 2
    z, xh = freq // 2, freq % 2
    pair_y = y + 1 - 2 * (y % 2)
    outer_y = 3 - y
    far_y = 3 - pair_y
    is_source = (y // 2) == xl
    is_relay = jnp.logical_not(is_source)
    other_col = col + 1 - 2 * core
    x_col = (1 - xl) * 2 + core
    x_freq = z * 2 + 1 - xh

    others = [((z + k) % 4) for k in (1, 3, 2)]
    z_devs = [(y, col, o * 2 + xh) for o in others]
    twin = (y, x_col, freq)
    cross = (y, x_col, x_freq)
    pair = (pair_y, col, freq)
    outer = (outer_y, col, freq)
    mate = (y, other_col, freq)

    barrier = pltpu.get_barrier_semaphore()
    peers = z_devs + [twin, cross, pair, outer, mate]

    def remote(src, dst, send, recv, peer):
        return pltpu.make_async_remote_copy(
            src_ref=src, dst_ref=dst, send_sem=send, recv_sem=recv,
            device_id=peer, device_id_type=MESH,
        )

    def slot_of(row_, col_=col):
        return jnp.where(row_ == col_, 2 + core, 4)

    def free(t, row_, i):
        return buf.at[t, jnp.where(row_ == col, 2, 4), 0, i]

    def piece(t, slot, k):
        a, b = {1: (1 - xl, xh), 2: (xl, 1 - xh), 3: (1 - xl, 1 - xh), 4: (xl, xh)}[k]
        return buf.at[t, slot, a, b]

    def send(t, index, src, dst, recv, peer):
        return remote(src, dst, sends.at[index], recvs.at[t, recv], peer).start()

    def z_sends(t):
        for j in range(6):
            dst = wbuf.at[t, z] if j % 2 else buf.at[t, core, xl, xh, z]
            send(t, j, mine.at[t, j], dst, Z, z_devs[j // 2])

    needs_r = jnp.logical_not(col == y)
    gives_r = jnp.logical_not(other_col == y)

    def same(t, index, place, recv, peer):
        send(t, index, place, place, recv, peer)

    def transform(rows):
        for peer in peers:
            pl.semaphore_signal(barrier, inc=1, device_id=peer, device_id_type=MESH)

        def whiten(w, spectrum):
            energy = jnp.sum(spectrum * spectrum, axis=0, keepdims=True) * (1.0 / SAMPLES)
            factor = mask_ref[pl.ds(w, 1), :].astype(jnp.float32) * lax.rsqrt(energy + EPSILON)
            rows[pl.ds(w, 2 * BINS, stride=NW), :] = spectrum * factor

        def one_chunk(i, carry):
            for j in range(NW // CHUNKS // 2):
                w = i * (NW // CHUNKS) + 2 * j
                one, two = traces_ref[w], traces_ref[w + 1]
                spare = LANES - NS
                both = jnp.concatenate([one, two[:spare], two, one[:spare]], axis=0)
                spectrum = lax.dot_general(
                    dft_ref[...], both, NT_DIMS, preferred_element_type=jnp.float32
                )
                whiten(w, spectrum[:, :NS])
                whiten(w + 1, spectrum[:, LANES : LANES + NS])
            return carry

        lax.fori_loop(0, CHUNKS, one_chunk, 0)
        pl.semaphore_wait(barrier, len(peers))

    def wait_only(ref, sem):
        pltpu.make_async_copy(ref, ref, sem).wait()

    r_slot = jnp.where(col == y, 0, 2)
    lane = lax.broadcasted_iota(jnp.int32, (1, LANES), 1)
    scale = 1.0 / math.sqrt(WINDOWS)

    def rows_of(t, slot, src):
        parts = [buf[t, slot + c % 2, c // 2, src // 4, src % 4] for c in range(4)]
        return jnp.concatenate(parts, axis=0)

    def roll(tile, by):
        return pltpu.roll(tile.astype(jnp.float32), by, 1)

    def masked(tile, ahead, back, lo, hi):
        inside = (lane >= lo) & (lane < hi)
        turned = jnp.where(lane < lo + NW, ahead, -back).astype(jnp.bfloat16)
        zero = jnp.zeros_like(tile)
        return jnp.where(inside, tile, zero), jnp.where(inside, turned, zero)

    def main(rows, lhs):
        def turn(t):
            for k in range(4):
                for i in range(2):
                    f = ((z + (0, 1, 3, 2)[k]) % 4) * 2 + (1 - xh if i else xh)
                    start = pl.multiple_of((f * NT + t) * LANES, LANES)
                    turned = rows[pl.ds(start, LANES), :].T.astype(jnp.bfloat16)
                    if k:
                        mine[t, 2 * (k - 1) + i] = turned
                    elif i:
                        wbuf[t, z] = turned
                    else:
                        buf[t, core, xl, xh, z] = turned
            z_sends(t)

        def put(k, tile, ahead, back, lo, hi):
            plain, turned = masked(tile, ahead, back, lo, hi)
            lhs[pl.ds(0, 4 * NS), pl.ds(k * LANES, LANES)] = plain
            lhs[pl.ds(4 * NS, 4 * NS), pl.ds(k * LANES, LANES)] = turned

        def store(b, rhs):
            product = lax.dot_general(
                lhs[:, pl.ds(0, LANES * len(rhs))], jnp.concatenate(rhs, axis=1), NT_DIMS,
                preferred_element_type=jnp.float32,
            )
            product = (product * scale).astype(jnp.bfloat16)
            out_ref[0, b] = product[: 4 * NS]
            out_ref[1, b] = product[4 * NS :]

        def whole_bin(t, b):
            lo = 2 * NW * b - LANES * t
            for s in range(8):
                tile = rows_of(t, 0, s)
                put(s, tile, roll(tile, LANES - NW), roll(tile, NW), lo, lo + 2 * NW)
            store(b, [rows_of(t, r_slot, s) for s in range(8)])

        def split_bin(t, b):
            lo = 2 * NW * b - LANES * t
            for s in range(8):
                before, tile = rows_of(t - 1, 0, s), rows_of(t, 0, s)
                ahead = roll(tile, LANES - NW)
                back = roll(before, NW)
                put(2 * s, before, jnp.where(lane < LANES - NW, roll(before, LANES - NW), ahead),
                    back, lo + LANES, LANES)
                put(2 * s + 1, tile, ahead, jnp.where(lane < NW, back, roll(tile, NW)),
                    lo, lo + 2 * NW)
            store(b, [rows_of(t - 1 + i, r_slot, s) for s in range(8) for i in range(2)])

        def multiply(t):
            first = (LANES * t) // (2 * NW)
            last = (LANES * (t + 1)) // (2 * NW)
            split = (t % PERIOD != 0).astype(jnp.int32)

            @pl.when(t % PERIOD != 0)
            def _():
                split_bin(t, first)

            def one(b, carry):
                whole_bin(t, b)
                return carry

            lax.fori_loop(first + split, last, one, 0)

        def own(t):
            wait_only(mine.at[t], recvs.at[t, Z])
            send(t, 6, wbuf.at[t], piece(t, core, 4), X1, cross)
            same(t, 7, piece(t, core, 4), CA, twin)

            @pl.when(is_source)
            def _():
                send(t, 11, piece(t, core, 4), piece(t, slot_of(y), 4), O4, outer)

            @pl.when(is_relay)
            def _():
                send(t, 11, wbuf.at[t], free(t, outer_y, 0), O4, outer)

        def twin_b(t):
            wait_only(piece(t, core, 3), recvs.at[t, X1])
            same(t, 8, piece(t, core, 3), CB, twin)

            @pl.when(is_source)
            def _():
                send(t, 12, piece(t, core, 3), piece(t, slot_of(y), 3), P1, pair)

        def send_a(t):
            wait_only(piece(t, core, 1), recvs.at[t, CA])

            @pl.when(is_source)
            def _():
                send(t, 13, piece(t, core, 1), piece(t, slot_of(y), 1), O1, outer)
                send(t, 14, piece(t, core, 1), piece(t, slot_of(y), 1), P1, pair)

        def send_b(t):
            wait_only(piece(t, core, 2), recvs.at[t, CB])

            @pl.when(is_source)
            def _():
                send(t, 15, piece(t, core, 2), piece(t, slot_of(y), 2), O2, outer)

            same(t, 9, buf.at[t, core], CL, mate)

        def relay(t, index, k, recv, recv_next):
            held = piece(t, slot_of(outer_y), k)
            wait_only(held, recvs.at[t, recv])
            same(t, index, held, recv_next, pair)

        def relay_a(t):
            @pl.when(is_relay)
            def _():
                relay(t, 12, 4, O4, P4)

            @pl.when(is_source)
            def _():
                held = free(t, y, 0)
                wait_only(held, recvs.at[t, O4])
                send(t, 16, held, free(t, pair_y, 1), P4, pair)
                dst = buf.at[t, slot_of(outer_y, x_col), xl, xh]
                send(t, 17, held, dst, XW, cross)

        def relay_b(t):
            @pl.when(is_relay)
            def _():
                relay(t, 13, 1, O1, P1)

        def relay_c(t):
            @pl.when(is_relay)
            def _():
                relay(t, 14, 2, O2, P2)

        def loop_a(t):
            @pl.when(is_relay)
            def _():
                held = piece(t, slot_of(far_y), 4)
                wait_only(held, recvs.at[t, P4])
                same(t, 15, held, O1, outer)

            @pl.when(is_source)
            def _():
                held = free(t, y, 1)
                wait_only(held, recvs.at[t, P4])
                send(t, 18, held, buf.at[t, slot_of(far_y, x_col), xl, xh], XW, cross)

        def loop_b(t):
            @pl.when(is_relay)
            def _():
                held = piece(t, slot_of(far_y), 2)
                wait_only(held, recvs.at[t, P2])
                same(t, 16, held, O1, outer)
                wait_only(piece(t, slot_of(far_y), 1), recvs.at[t, P1])

        def both_rows(t):
            @pl.when(is_relay)
            def _():
                wait_only(buf.at[t, 4, xl], recvs.at[t, XW])

            @pl.when(is_source)
            def _():
                wait_only(buf.at[t, slot_of(pair_y), 1 - xl], recvs.at[t, P1])
                wait_only(buf.at[t, slot_of(pair_y), xl], recvs.at[t, O1])

            @pl.when(gives_r)
            def _():
                send(t, 10, buf.at[t, 4], buf.at[t, 2 + core], CR, mate)

        def products(t):
            wait_only(buf.at[t, 1 - core], recvs.at[t, CL])

            @pl.when(needs_r)
            def _():
                wait_only(buf.at[t, 3 - core], recvs.at[t, CR])

            multiply(t)

        events = {
            "own": own, "turn": turn, "loop_b": loop_b, "relay_a": relay_a, "twin_b": twin_b,
            "send_a": send_a, "loop_a": loop_a, "relay_b": relay_b, "multiply": products,
            "send_b": send_b, "relay_c": relay_c, "rows": both_rows,
        }

        def step(tau, carry):
            for name, lag in ORDER:
                @pl.when(jnp.logical_and(tau >= lag, tau < NT + lag))
                def _():
                    events[name](tau - lag)

            return carry

        for t in range(-dict(ORDER)["turn"]):
            turn(t)
        lax.fori_loop(0, NT + dict(ORDER)["multiply"], step, 0)

    def stages(rows):
        transform(rows)
        pl.run_scoped(
            lambda lhs: main(rows, lhs), pltpu.VMEM((8 * NS, 16 * LANES), jnp.bfloat16)
        )

    pl.run_scoped(stages, pltpu.VMEM((2 * BINS * NW, NS), jnp.float32))

    one, two = wbuf, buf.at[:, core]
    for j in range(6):
        wait_only(mine.at[:, j], sends.at[j])
    for j in (6, 7, 8, 11, 12, 13, 14, 15, 16):
        wait_only(one, sends.at[j])
    wait_only(two, sends.at[9])

    @pl.when(gives_r)
    def _():
        wait_only(two, sends.at[10])

    @pl.when(is_source)
    def _():
        for j in (17, 18):
            wait_only(one, sends.at[j])


def shards(traces, window_mask):
    dft = jnp.asarray(dft_table().astype(jnp.bfloat16))
    dma = pltpu.SemaphoreType.DMA
    bf16 = jnp.bfloat16
    return pl.pallas_call(
        kernel,
        out_shape=jax.ShapeDtypeStruct((2, 32, 320, 320), bf16),
        in_specs=[pl.BlockSpec(memory_space=pltpu.VMEM)] * 3,
        out_specs=pl.BlockSpec(memory_space=pltpu.VMEM),
        scratch_shapes=[
            pltpu.VMEM((NT, 6, NS, LANES), bf16),
            pltpu.VMEM((NT, 4, NS, LANES), bf16),
            pltpu.VMEM((NT, 5, 2, 2, 4, NS, LANES), bf16),
            dma((19,)), dma((NT, 13)),
        ],
        compiler_params=pltpu.CompilerParams(
            collective_id=0, has_side_effects=True, vmem_limit_bytes=36 * 2**20
        ),
        cost_estimate=pl.CostEstimate(
            flops=12 * 10**9, bytes_accessed=20 * 10**6, transcendentals=0
        ),
        name="cross_spectra",
    )(dft, jnp.transpose(traces, (1, 0, 2)), jnp.transpose(window_mask))


def solution(mesh):
    placed = (P(("row", "col"), "freq", None), P(("row", "col"), "freq"))
    return jax.shard_map(
        shards, mesh=mesh, in_specs=placed, out_specs=P(None, "freq", "row", "col"), check_vma=False
    )
```

```python
import math

import jax
import jax.numpy as jnp
import numpy as np
from jax import lax
from jax.experimental import pallas as pl
from jax.experimental.pallas import tpu as pltpu
from jax.sharding import PartitionSpec as P

SAMPLES = 512
BINS = 256
EPSILON = 1e-06
NS = 80
NW = 28
LANES = 128
NT = 14
PERIOD = 7
CHUNKS = 2
WINDOWS = 224
MESH = pl.DeviceIdType.MESH
NT_DIMS = (((1,), (1,)), ((), ()))

ORDER = (
    ("own", 0), ("turn", -3), ("loop_b", 5), ("relay_a", 1), ("twin_b", 1), ("send_a", 2),
    ("loop_a", 3), ("relay_b", 3), ("multiply", 7), ("send_b", 2), ("relay_c", 3), ("rows", 5),
)
Z, X1, CA, CB, CL, CR, O4, O1, O2, P4, P1, P2, XW = range(13)


def dft_table():
    t = np.arange(SAMPLES, dtype=np.int64)
    k = np.arange(BINS, dtype=np.int64)
    angles = 2.0 * math.pi / SAMPLES * ((k[:, None] * t[None, :]) % SAMPLES)
    taper = 0.5 - 0.5 * np.cos(2.0 * math.pi / SAMPLES * t)
    stacked = np.stack([taper * np.cos(angles), -taper * np.sin(angles)], axis=1)
    return stacked.reshape(2 * BINS, SAMPLES).astype(np.float32)


def kernel(
    dft_ref, traces_ref, mask_ref, out_ref, mine, wbuf, buf, sends, recvs,
):
    y = lax.axis_index("row")
    col = lax.axis_index("col")
    freq = lax.axis_index("freq")
    xl, core = col // 2, col % 2
    z, xh = freq // 2, freq % 2
    pair_y = y + 1 - 2 * (y % 2)
    outer_y = 3 - y
    far_y = 3 - pair_y
    is_source = (y // 2) == xl
    is_relay = jnp.logical_not(is_source)
    other_col = col + 1 - 2 * core
    x_col = (1 - xl) * 2 + core
    x_freq = z * 2 + 1 - xh

    others = [((z + k) % 4) for k in (1, 3, 2)]
    z_devs = [(y, col, o * 2 + xh) for o in others]
    twin = (y, x_col, freq)
    cross = (y, x_col, x_freq)
    pair = (pair_y, col, freq)
    outer = (outer_y, col, freq)
    mate = (y, other_col, freq)

    barrier = pltpu.get_barrier_semaphore()
    peers = z_devs + [twin, cross, pair, outer, mate]

    def remote(src, dst, send, recv, peer):
        return pltpu.make_async_remote_copy(
            src_ref=src, dst_ref=dst, send_sem=send, recv_sem=recv,
            device_id=peer, device_id_type=MESH,
        )

    def slot_of(row_, col_=col):
        return jnp.where(row_ == col_, 2 + core, 4)

    def free(t, row_, i):
        return buf.at[t, jnp.where(row_ == col, 2, 4), 0, i]

    def piece(t, slot, k):
        a, b = {1: (1 - xl, xh), 2: (xl, 1 - xh), 3: (1 - xl, 1 - xh), 4: (xl, xh)}[k]
        return buf.at[t, slot, a, b]

    def send(t, index, src, dst, recv, peer):
        return remote(src, dst, sends.at[index], recvs.at[t, recv], peer).start()

    def z_sends(t):
        for j in range(6):
            dst = wbuf.at[t, z] if j % 2 else buf.at[t, core, xl, xh, z]
            send(t, j, mine.at[t, j], dst, Z, z_devs[j // 2])

    needs_r = jnp.logical_not(col == y)
    gives_r = jnp.logical_not(other_col == y)

    def same(t, index, place, recv, peer):
        send(t, index, place, place, recv, peer)

    def transform(rows):
        for peer in peers:
            pl.semaphore_signal(barrier, inc=1, device_id=peer, device_id_type=MESH)

        def whiten(w, spectrum):
            energy = jnp.sum(spectrum * spectrum, axis=0, keepdims=True) * (1.0 / SAMPLES)
            factor = mask_ref[pl.ds(w, 1), :].astype(jnp.float32) * lax.rsqrt(energy + EPSILON)
            rows[pl.ds(w, 2 * BINS, stride=NW), :] = spectrum * factor

        def one_chunk(i, carry):
            for j in range(NW // CHUNKS // 2):
                w = i * (NW // CHUNKS) + 2 * j
                one, two = traces_ref[w], traces_ref[w + 1]
                spare = LANES - NS
                both = jnp.concatenate([one, two[:spare], two, one[:spare]], axis=0)
                spectrum = lax.dot_general(
                    dft_ref[...], both, NT_DIMS, preferred_element_type=jnp.float32
                )
                whiten(w, spectrum[:, :NS])
                whiten(w + 1, spectrum[:, LANES : LANES + NS])
            return carry

        lax.fori_loop(0, CHUNKS, one_chunk, 0)
        pl.semaphore_wait(barrier, len(peers))

    def wait_only(ref, sem):
        pltpu.make_async_copy(ref, ref, sem).wait()

    r_slot = jnp.where(col == y, 0, 2)
    lane = lax.broadcasted_iota(jnp.int32, (1, LANES), 1)
    scale = 1.0 / math.sqrt(WINDOWS)

    def rows_of(t, slot, src):
        parts = [buf[t, slot + c % 2, c // 2, src // 4, src % 4] for c in range(4)]
        return jnp.concatenate(parts, axis=0)

    def fold(t, slot, pair, lo, split):
        tiles = []
        for src in (2 * pair, 2 * pair + 1):
            tile = rows_of(t, slot, src)
            if split:
                tile = jnp.where(lane >= lo + LANES, rows_of(t - 1, slot, src), tile)
            tiles.append(tile)
        return jnp.where(place(lo) < LANES // 2, tiles[0], pltpu.roll(tiles[1], LANES // 2, 1))

    def place(lo):
        return (lane - lo + LANES) % LANES

    def main(rows, lhs):
        def turn(t):
            for k in range(4):
                for i in range(2):
                    f = ((z + (0, 1, 3, 2)[k]) % 4) * 2 + (1 - xh if i else xh)
                    start = pl.multiple_of((f * NT + t) * LANES, LANES)
                    turned = rows[pl.ds(start, LANES), :].T.astype(jnp.bfloat16)
                    if k:
                        mine[t, 2 * (k - 1) + i] = turned
                    elif i:
                        wbuf[t, z] = turned
                    else:
                        buf[t, core, xl, xh, z] = turned
            z_sends(t)

        def one_bin(t, b, split):
            lo = 2 * NW * b - LANES * t
            half = place(lo) % (LANES // 2)
            for pair in range(4):
                tile = fold(t, 0, pair, lo, split)
                ahead = pltpu.roll(tile, LANES - NW, 1)
                back = pltpu.roll(tile, NW, 1)
                turned = jnp.where(half < NW, ahead, -back)
                zero = jnp.zeros_like(tile)
                part = pl.ds(pair * LANES, LANES)
                lhs[pl.ds(0, 4 * NS), part] = jnp.where(half < 2 * NW, tile, zero)
                lhs[pl.ds(4 * NS, 4 * NS), part] = jnp.where(half < 2 * NW, turned, zero)
            rhs = jnp.concatenate([fold(t, r_slot, pair, lo, split) for pair in range(4)], axis=1)
            product = lax.dot_general(
                lhs[...], rhs, NT_DIMS, preferred_element_type=jnp.float32
            )
            product = (product * scale).astype(jnp.bfloat16)
            out_ref[0, b] = product[: 4 * NS]
            out_ref[1, b] = product[4 * NS :]

        def multiply(t):
            first = (LANES * t) // (2 * NW)
            last = (LANES * (t + 1)) // (2 * NW)
            split = (t % PERIOD != 0).astype(jnp.int32)

            @pl.when(t % PERIOD != 0)
            def _():
                one_bin(t, first, True)

            def one(b, carry):
                one_bin(t, b, False)
                return carry

            lax.fori_loop(first + split, last, one, 0)

        def own(t):
            wait_only(mine.at[t], recvs.at[t, Z])
            send(t, 6, wbuf.at[t], piece(t, core, 4), X1, cross)
            same(t, 7, piece(t, core, 4), CA, twin)

            @pl.when(is_source)
            def _():
                send(t, 11, piece(t, core, 4), piece(t, slot_of(y), 4), O4, outer)

            @pl.when(is_relay)
            def _():
                send(t, 11, wbuf.at[t], free(t, outer_y, 0), O4, outer)

        def twin_b(t):
            wait_only(piece(t, core, 3), recvs.at[t, X1])
            same(t, 8, piece(t, core, 3), CB, twin)

            @pl.when(is_source)
            def _():
                send(t, 12, piece(t, core, 3), piece(t, slot_of(y), 3), P1, pair)

        def send_a(t):
            wait_only(piece(t, core, 1), recvs.at[t, CA])

            @pl.when(is_source)
            def _():
                send(t, 13, piece(t, core, 1), piece(t, slot_of(y), 1), O1, outer)
                send(t, 14, piece(t, core, 1), piece(t, slot_of(y), 1), P1, pair)

        def send_b(t):
            wait_only(piece(t, core, 2), recvs.at[t, CB])

            @pl.when(is_source)
            def _():
                send(t, 15, piece(t, core, 2), piece(t, slot_of(y), 2), O2, outer)

            same(t, 9, buf.at[t, core], CL, mate)

        def relay(t, index, k, recv, recv_next):
            held = piece(t, slot_of(outer_y), k)
            wait_only(held, recvs.at[t, recv])
            same(t, index, held, recv_next, pair)

        def relay_a(t):
            @pl.when(is_relay)
            def _():
                relay(t, 12, 4, O4, P4)

            @pl.when(is_source)
            def _():
                held = free(t, y, 0)
                wait_only(held, recvs.at[t, O4])
                send(t, 16, held, free(t, pair_y, 1), P4, pair)
                dst = buf.at[t, slot_of(outer_y, x_col), xl, xh]
                send(t, 17, held, dst, XW, cross)

        def relay_b(t):
            @pl.when(is_relay)
            def _():
                relay(t, 13, 1, O1, P1)

        def relay_c(t):
            @pl.when(is_relay)
            def _():
                relay(t, 14, 2, O2, P2)

        def loop_a(t):
            @pl.when(is_relay)
            def _():
                held = piece(t, slot_of(far_y), 4)
                wait_only(held, recvs.at[t, P4])
                same(t, 15, held, O1, outer)

            @pl.when(is_source)
            def _():
                held = free(t, y, 1)
                wait_only(held, recvs.at[t, P4])
                send(t, 18, held, buf.at[t, slot_of(far_y, x_col), xl, xh], XW, cross)

        def loop_b(t):
            @pl.when(is_relay)
            def _():
                held = piece(t, slot_of(far_y), 2)
                wait_only(held, recvs.at[t, P2])
                same(t, 16, held, O1, outer)
                wait_only(piece(t, slot_of(far_y), 1), recvs.at[t, P1])

        def both_rows(t):
            @pl.when(is_relay)
            def _():
                wait_only(buf.at[t, 4, xl], recvs.at[t, XW])

            @pl.when(is_source)
            def _():
                wait_only(buf.at[t, slot_of(pair_y), 1 - xl], recvs.at[t, P1])
                wait_only(buf.at[t, slot_of(pair_y), xl], recvs.at[t, O1])

            @pl.when(gives_r)
            def _():
                send(t, 10, buf.at[t, 4], buf.at[t, 2 + core], CR, mate)

        def products(t):
            wait_only(buf.at[t, 1 - core], recvs.at[t, CL])

            @pl.when(needs_r)
            def _():
                wait_only(buf.at[t, 3 - core], recvs.at[t, CR])

            multiply(t)

        events = {
            "own": own, "turn": turn, "loop_b": loop_b, "relay_a": relay_a, "twin_b": twin_b,
            "send_a": send_a, "loop_a": loop_a, "relay_b": relay_b, "multiply": products,
            "send_b": send_b, "relay_c": relay_c, "rows": both_rows,
        }

        def step(tau, carry):
            for name, lag in ORDER:
                @pl.when(jnp.logical_and(tau >= lag, tau < NT + lag))
                def _():
                    events[name](tau - lag)

            return carry

        for t in range(-dict(ORDER)["turn"]):
            turn(t)
        lax.fori_loop(0, NT + dict(ORDER)["multiply"], step, 0)

    def stages(rows):
        transform(rows)
        pl.run_scoped(
            lambda lhs: main(rows, lhs), pltpu.VMEM((8 * NS, 4 * LANES), jnp.bfloat16)
        )

    pl.run_scoped(stages, pltpu.VMEM((2 * BINS * NW, NS), jnp.float32))

    one, two = wbuf, buf.at[:, core]
    for j in range(6):
        wait_only(mine.at[:, j], sends.at[j])
    for j in (6, 7, 8, 11, 12, 13, 14, 15, 16):
        wait_only(one, sends.at[j])
    wait_only(two, sends.at[9])

    @pl.when(gives_r)
    def _():
        wait_only(two, sends.at[10])

    @pl.when(is_source)
    def _():
        for j in (17, 18):
            wait_only(one, sends.at[j])


def shards(traces, window_mask):
    dft = jnp.asarray(dft_table().astype(jnp.bfloat16))
    dma = pltpu.SemaphoreType.DMA
    bf16 = jnp.bfloat16
    return pl.pallas_call(
        kernel,
        out_shape=jax.ShapeDtypeStruct((2, 32, 320, 320), bf16),
        in_specs=[pl.BlockSpec(memory_space=pltpu.VMEM)] * 3,
        out_specs=pl.BlockSpec(memory_space=pltpu.VMEM),
        scratch_shapes=[
            pltpu.VMEM((NT, 6, NS, LANES), bf16),
            pltpu.VMEM((NT, 4, NS, LANES), bf16),
            pltpu.VMEM((NT, 5, 2, 2, 4, NS, LANES), bf16),
            dma((19,)), dma((NT, 13)),
        ],
        compiler_params=pltpu.CompilerParams(
            collective_id=0, has_side_effects=True, vmem_limit_bytes=36 * 2**20
        ),
        cost_estimate=pl.CostEstimate(
            flops=12 * 10**9, bytes_accessed=20 * 10**6, transcendentals=0
        ),
        name="cross_spectra",
    )(dft, jnp.transpose(traces, (1, 0, 2)), jnp.transpose(window_mask))


def solution(mesh):
    placed = (P(("row", "col"), "freq", None), P(("row", "col"), "freq"))
    return jax.shard_map(
        shards, mesh=mesh, in_specs=placed, out_specs=P(None, "freq", "row", "col"), check_vma=False
    )
```

```python
import math

import jax
import jax.numpy as jnp
import numpy as np
from jax import lax
from jax.experimental import pallas as pl
from jax.experimental.pallas import tpu as pltpu
from jax.sharding import PartitionSpec as P

SAMPLES = 512
BINS = 256
EPSILON = 1e-06
NS = 80
NW = 28
LANES = 128
NT = 14
PERIOD = 7
CHUNKS = 2
WINDOWS = 224
MESH = pl.DeviceIdType.MESH
NT_DIMS = (((1,), (1,)), ((), ()))

ORDER = (
    ("T", "own_t", 0),
    ("S", "next_outer", 2),
    ("S", "whole_s", 3),
    ("T", "relay_4", 1),
    ("T", "near_t", 1),
    ("B", "products", 6),
    ("T", "relay_1", 2),
    ("T", "loop_1", 3),
    ("B", "turn", -2),
    ("T", "loop_4", 2),
    ("S", "near_s", 2),
    ("T", "twin_a_t", 1),
    ("T", "whole_t", 3),
    ("T", "relay_2", 3),
    ("S", "own_s", 0),
    ("S", "twin_a_s", 1),
    ("S", "next_far", 3),
    ("T", "rows_t", 4),
    ("S", "rows_s", 4),
)
Z, X1, CA, CB, CL, CR, O4, O1, O2, P4, P1, P2, XW = range(13)


def dft_table():
    t = np.arange(SAMPLES, dtype=np.int64)
    k = np.arange(BINS, dtype=np.int64)
    angles = 2.0 * math.pi / SAMPLES * ((k[:, None] * t[None, :]) % SAMPLES)
    taper = 0.5 - 0.5 * np.cos(2.0 * math.pi / SAMPLES * t)
    stacked = np.stack([taper * np.cos(angles), -taper * np.sin(angles)], axis=1)
    return stacked.reshape(2 * BINS, SAMPLES).astype(np.float32)


def kernel(
    dft_ref, traces_ref, mask_ref, out_ref, mine, wbuf, buf, sends, recvs,
):
    y = lax.axis_index("row")
    col = lax.axis_index("col")
    freq = lax.axis_index("freq")
    xl, core = col // 2, col % 2
    z, xh = freq // 2, freq % 2
    pair_y = y + 1 - 2 * (y % 2)
    outer_y = 3 - y
    far_y = 3 - pair_y
    is_source = (y // 2) == xl
    is_relay = jnp.logical_not(is_source)
    other_col = col + 1 - 2 * core
    x_col = (1 - xl) * 2 + core
    x_freq = z * 2 + 1 - xh

    others = [((z + k) % 4) for k in (1, 3, 2)]
    z_devs = [(y, col, o * 2 + xh) for o in others]
    twin = (y, x_col, freq)
    cross = (y, x_col, x_freq)
    pair = (pair_y, col, freq)
    outer = (outer_y, col, freq)
    mate = (y, other_col, freq)

    barrier = pltpu.get_barrier_semaphore()
    peers = z_devs + [twin, cross, pair, outer, mate]

    def remote(src, dst, send, recv, peer):
        return pltpu.make_async_remote_copy(
            src_ref=src, dst_ref=dst, send_sem=send, recv_sem=recv,
            device_id=peer, device_id_type=MESH,
        )

    def slot_of(row_, col_=col):
        return jnp.where(row_ == col_, 2 + core, 4)

    def free(t, row_, i):
        return buf.at[t, jnp.where(row_ == col, 2, 4), 0, i]

    def piece(t, slot, k):
        a, b = {1: (1 - xl, xh), 2: (xl, 1 - xh), 3: (1 - xl, 1 - xh), 4: (xl, xh)}[k]
        return buf.at[t, slot, a, b]

    def send(t, index, src, dst, recv, peer):
        return remote(src, dst, sends.at[index], recvs.at[t, recv], peer).start()

    def z_sends(t):
        for j in range(6):
            dst = wbuf.at[t, z] if j % 2 else buf.at[t, core, xl, xh, z]
            send(t, j, mine.at[t, j], dst, Z, z_devs[j // 2])

    needs_r = jnp.logical_not(col == y)
    gives_r = jnp.logical_not(other_col == y)

    def same(t, index, place, recv, peer):
        send(t, index, place, place, recv, peer)

    def transform(rows):
        for peer in peers:
            pl.semaphore_signal(barrier, inc=1, device_id=peer, device_id_type=MESH)

        def whiten(w, spectrum):
            energy = jnp.sum(spectrum * spectrum, axis=0, keepdims=True) * (1.0 / SAMPLES)
            factor = mask_ref[pl.ds(w, 1), :].astype(jnp.float32) * lax.rsqrt(energy + EPSILON)
            rows[pl.ds(w, 2 * BINS, stride=NW), :] = spectrum * factor

        def one_chunk(i, carry):
            for j in range(NW // CHUNKS // 2):
                w = i * (NW // CHUNKS) + 2 * j
                one, two = traces_ref[w], traces_ref[w + 1]
                spare = LANES - NS
                both = jnp.concatenate([one, two[:spare], two, one[:spare]], axis=0)
                spectrum = lax.dot_general(
                    dft_ref[...], both, NT_DIMS, preferred_element_type=jnp.float32
                )
                whiten(w, spectrum[:, :NS])
                whiten(w + 1, spectrum[:, LANES : LANES + NS])
            return carry

        lax.fori_loop(0, CHUNKS, one_chunk, 0)
        pl.semaphore_wait(barrier, len(peers))

    def wait_only(ref, sem):
        pltpu.make_async_copy(ref, ref, sem).wait()

    r_slot = jnp.where(col == y, 0, 2)
    lane = lax.broadcasted_iota(jnp.int32, (1, LANES), 1)
    scale = 1.0 / math.sqrt(WINDOWS)

    def rows_of(t, slot, src):
        parts = [buf[t, slot + c % 2, c // 2, src // 4, src % 4] for c in range(4)]
        return jnp.concatenate(parts, axis=0)

    def fold(t, slot, pair, lo, split):
        tiles = []
        for src in (2 * pair, 2 * pair + 1):
            tile = rows_of(t, slot, src)
            if split:
                tile = jnp.where(lane >= lo + LANES, rows_of(t - 1, slot, src), tile)
            tiles.append(tile)
        return jnp.where(place(lo) < LANES // 2, tiles[0], pltpu.roll(tiles[1], LANES // 2, 1))

    def place(lo):
        return (lane - lo + LANES) % LANES

    def main(rows, lhs):
        def turn(t):
            for k in range(4):
                for i in range(2):
                    f = ((z + (0, 1, 3, 2)[k]) % 4) * 2 + (1 - xh if i else xh)
                    start = pl.multiple_of((f * NT + t) * LANES, LANES)
                    turned = rows[pl.ds(start, LANES), :].T.astype(jnp.bfloat16)
                    if k:
                        mine[t, 2 * (k - 1) + i] = turned
                    elif i:
                        wbuf[t, z] = turned
                    else:
                        buf[t, core, xl, xh, z] = turned
            z_sends(t)

        def one_bin(t, b, split):
            lo = 2 * NW * b - LANES * t
            half = place(lo) % (LANES // 2)
            for pair in range(4):
                tile = fold(t, 0, pair, lo, split)
                ahead = pltpu.roll(tile, LANES - NW, 1)
                back = pltpu.roll(tile, NW, 1)
                turned = jnp.where(half < NW, ahead, -back)
                zero = jnp.zeros_like(tile)
                part = pl.ds(pair * LANES, LANES)
                lhs[pl.ds(0, 4 * NS), part] = jnp.where(half < 2 * NW, tile, zero)
                lhs[pl.ds(4 * NS, 4 * NS), part] = jnp.where(half < 2 * NW, turned, zero)
            rhs = jnp.concatenate([fold(t, r_slot, pair, lo, split) for pair in range(4)], axis=1)
            product = lax.dot_general(
                lhs[...], rhs, NT_DIMS, preferred_element_type=jnp.float32
            )
            product = (product * scale).astype(jnp.bfloat16)
            out_ref[0, b] = product[: 4 * NS]
            out_ref[1, b] = product[4 * NS :]

        def multiply(t):
            first = (LANES * t) // (2 * NW)
            last = (LANES * (t + 1)) // (2 * NW)
            split = (t % PERIOD != 0).astype(jnp.int32)

            @pl.when(t % PERIOD != 0)
            def _():
                one_bin(t, first, True)

            def one(b, carry):
                one_bin(t, b, False)
                return carry

            lax.fori_loop(first + split, last, one, 0)

        def own(t):
            wait_only(mine.at[t], recvs.at[t, Z])
            send(t, 6, wbuf.at[t], piece(t, core, 4), X1, cross)
            same(t, 7, piece(t, core, 4), CA, twin)

        def own_s(t):
            own(t)
            send(t, 11, piece(t, core, 4), piece(t, slot_of(y), 4), O4, outer)

        def own_t(t):
            own(t)
            send(t, 11, wbuf.at[t], free(t, outer_y, 0), O4, outer)

        def near(t):
            wait_only(piece(t, core, 3), recvs.at[t, X1])
            same(t, 8, piece(t, core, 3), CB, twin)

        def near_s(t):
            near(t)
            send(t, 12, piece(t, core, 3), piece(t, slot_of(y), 3), P2, pair)

        def twin_a(t):
            wait_only(piece(t, core, 1), recvs.at[t, CA])

        def twin_a_s(t):
            twin_a(t)
            send(t, 13, piece(t, core, 1), piece(t, slot_of(y), 1), O1, outer)

        def whole(t):
            wait_only(piece(t, core, 2), recvs.at[t, CB])

        def whole_s(t):
            whole(t)
            send(t, 15, piece(t, core, 2), piece(t, slot_of(y), 2), O2, outer)
            send(t, 14, piece(t, core, 2), piece(t, slot_of(y), 2), P2, pair)
            same(t, 9, buf.at[t, core], CL, mate)

        def whole_t(t):
            whole(t)
            same(t, 9, buf.at[t, core], CL, mate)

        def relay(t, index, k, recv, recv_next):
            held = piece(t, slot_of(outer_y), k)
            wait_only(held, recvs.at[t, recv])
            same(t, index, held, recv_next, pair)

        def relay_4(t):
            relay(t, 12, 4, O4, P4)

        def relay_1(t):
            relay(t, 13, 1, O1, P1)

        def relay_2(t):
            relay(t, 14, 2, O2, P2)

        def next_outer(t):
            held = free(t, y, 0)
            wait_only(held, recvs.at[t, O4])
            send(t, 16, held, free(t, pair_y, 1), P4, pair)
            send(t, 17, held, buf.at[t, slot_of(outer_y, x_col), xl, xh], XW, cross)

        def next_far(t):
            held = free(t, y, 1)
            wait_only(held, recvs.at[t, P4])
            send(t, 18, held, buf.at[t, slot_of(far_y, x_col), xl, xh], XW, cross)

        def loop(t, index, k, recv):
            held = piece(t, slot_of(far_y), k)
            wait_only(held, recvs.at[t, recv])
            same(t, index, held, O1, outer)

        def loop_4(t):
            loop(t, 15, 4, P4)

        def loop_1(t):
            loop(t, 16, 1, P1)

        def give(t):
            @pl.when(gives_r)
            def _():
                send(t, 10, buf.at[t, 4], buf.at[t, 2 + core], CR, mate)

        def rows_s(t):
            wait_only(buf.at[t, 4, xl], recvs.at[t, P2])
            wait_only(buf.at[t, 4, xl], recvs.at[t, O1])
            give(t)

        def rows_t(t):
            wait_only(piece(t, slot_of(far_y), 2), recvs.at[t, P2])
            wait_only(buf.at[t, 4, xl], recvs.at[t, XW])
            give(t)

        def products(t):
            wait_only(buf.at[t, 1 - core], recvs.at[t, CL])

            @pl.when(needs_r)
            def _():
                wait_only(buf.at[t, 3 - core], recvs.at[t, CR])

            multiply(t)

        events = {
            "turn": turn, "products": products,
            "own_s": own_s, "near_s": near_s, "twin_a_s": twin_a_s, "whole_s": whole_s,
            "next_outer": next_outer, "next_far": next_far, "rows_s": rows_s,
            "own_t": own_t, "near_t": near, "twin_a_t": twin_a, "whole_t": whole_t,
            "relay_4": relay_4, "relay_1": relay_1, "relay_2": relay_2,
            "loop_4": loop_4, "loop_1": loop_1, "rows_t": rows_t,
        }

        def step(tau, carry):
            for who, name, lag in ORDER:
                run = jnp.logical_and(tau >= lag, tau < NT + lag)
                if who != "B":
                    run = jnp.logical_and(run, is_source if who == "S" else is_relay)

                @pl.when(run)
                def _():
                    events[name](tau - lag)

            return carry

        lags = {name: lag for _, name, lag in ORDER}
        for t in range(-lags["turn"]):
            turn(t)
        lax.fori_loop(0, NT + max(lags.values()), step, 0)

    def stages(rows):
        transform(rows)
        pl.run_scoped(
            lambda lhs: main(rows, lhs), pltpu.VMEM((8 * NS, 4 * LANES), jnp.bfloat16)
        )

    pl.run_scoped(stages, pltpu.VMEM((2 * BINS * NW, NS), jnp.float32))

    one, two = wbuf, buf.at[:, core]
    for j in range(6):
        wait_only(mine.at[:, j], sends.at[j])
    for j in (6, 7, 8, 11, 12, 13, 14, 15, 16):
        wait_only(one, sends.at[j])
    wait_only(two, sends.at[9])

    @pl.when(gives_r)
    def _():
        wait_only(two, sends.at[10])

    @pl.when(is_source)
    def _():
        for j in (17, 18):
            wait_only(one, sends.at[j])


def shards(traces, window_mask):
    dft = jnp.asarray(dft_table().astype(jnp.bfloat16))
    dma = pltpu.SemaphoreType.DMA
    bf16 = jnp.bfloat16
    return pl.pallas_call(
        kernel,
        out_shape=jax.ShapeDtypeStruct((2, 32, 320, 320), bf16),
        in_specs=[pl.BlockSpec(memory_space=pltpu.VMEM)] * 3,
        out_specs=pl.BlockSpec(memory_space=pltpu.VMEM),
        scratch_shapes=[
            pltpu.VMEM((NT, 6, NS, LANES), bf16),
            pltpu.VMEM((NT, 4, NS, LANES), bf16),
            pltpu.VMEM((NT, 5, 2, 2, 4, NS, LANES), bf16),
            dma((19,)), dma((NT, 13)),
        ],
        compiler_params=pltpu.CompilerParams(
            collective_id=0, has_side_effects=True, vmem_limit_bytes=36 * 2**20
        ),
        cost_estimate=pl.CostEstimate(
            flops=12 * 10**9, bytes_accessed=20 * 10**6, transcendentals=0
        ),
        name="cross_spectra",
    )(dft, jnp.transpose(traces, (1, 0, 2)), jnp.transpose(window_mask))


def solution(mesh):
    placed = (P(("row", "col"), "freq", None), P(("row", "col"), "freq"))
    return jax.shard_map(
        shards, mesh=mesh, in_specs=placed, out_specs=P(None, "freq", "row", "col"), check_vma=False
    )
```

```python
import functools
import math

import jax
import jax.numpy as jnp
import numpy as np
from jax import lax
from jax.experimental import pallas as pl
from jax.experimental.pallas import tpu as pltpu
from jax.sharding import PartitionSpec as P

SAMPLES = 512
BINS = 256
EPSILON = 1e-06
NS = 80
NW = 28
LANES = 128
NT = 14
PERIOD = 7
CHUNKS = 2
WINDOWS = 224
MESH = pl.DeviceIdType.MESH
NT_DIMS = (((1,), (1,)), ((), ()))

ORDER = (
    ("T", "own_t", 0),
    ("S", "next_outer", 2),
    ("S", "whole_s", 3),
    ("T", "relay_4", 1),
    ("T", "near_t", 1),
    ("B", "products", 6),
    ("T", "relay_1", 2),
    ("T", "loop_1", 3),
    ("B", "turn", -2),
    ("T", "loop_4", 2),
    ("S", "near_s", 2),
    ("T", "twin_a_t", 1),
    ("T", "whole_t", 3),
    ("T", "relay_2", 3),
    ("S", "own_s", 0),
    ("S", "twin_a_s", 1),
    ("S", "next_far", 3),
    ("T", "rows_t", 4),
    ("S", "rows_s", 4),
)
Z, X1, CA, CB, CL, CR, O4, O1, O2, P4, P1, P2, XW = range(13)


def dft_table():
    t = np.arange(SAMPLES, dtype=np.int64)
    k = np.arange(BINS, dtype=np.int64)
    angles = 2.0 * math.pi / SAMPLES * ((k[:, None] * t[None, :]) % SAMPLES)
    taper = 0.5 - 0.5 * np.cos(2.0 * math.pi / SAMPLES * t)
    stacked = np.stack([taper * np.cos(angles), -taper * np.sin(angles)], axis=1)
    return stacked.reshape(2 * BINS, SAMPLES).astype(np.float32)


def kernel(
    dft_hbm, traces_hbm, mask_hbm, out_ref, mine, wbuf, buf, inputs, sends, recvs,
):
    y = lax.axis_index("row")
    col = lax.axis_index("col")
    freq = lax.axis_index("freq")
    xl, core = col // 2, col % 2
    z, xh = freq // 2, freq % 2
    pair_y = y + 1 - 2 * (y % 2)
    outer_y = 3 - y
    far_y = 3 - pair_y
    is_source = (y // 2) == xl
    is_relay = jnp.logical_not(is_source)
    other_col = col + 1 - 2 * core
    x_col = (1 - xl) * 2 + core
    x_freq = z * 2 + 1 - xh

    others = [((z + k) % 4) for k in (1, 3, 2)]
    z_devs = [(y, col, o * 2 + xh) for o in others]
    twin = (y, x_col, freq)
    cross = (y, x_col, x_freq)
    pair = (pair_y, col, freq)
    outer = (outer_y, col, freq)
    mate = (y, other_col, freq)

    barrier = pltpu.get_barrier_semaphore()
    peers = z_devs + [twin, cross, pair, outer, mate]

    def remote(src, dst, send, recv, peer):
        return pltpu.make_async_remote_copy(
            src_ref=src, dst_ref=dst, send_sem=send, recv_sem=recv,
            device_id=peer, device_id_type=MESH,
        )

    def slot_of(row_, col_=col):
        return jnp.where(row_ == col_, 2 + core, 4)

    def free(t, row_, i):
        return buf.at[t, jnp.where(row_ == col, 2, 4), 0, i]

    def piece(t, slot, k):
        a, b = {1: (1 - xl, xh), 2: (xl, 1 - xh), 3: (1 - xl, 1 - xh), 4: (xl, xh)}[k]
        return buf.at[t, slot, a, b]

    def send(t, index, src, dst, recv, peer):
        return remote(src, dst, sends.at[index], recvs.at[t, recv], peer).start()

    def z_sends(t):
        for j in range(6):
            dst = wbuf.at[t, z] if j % 2 else buf.at[t, core, xl, xh, z]
            send(t, j, mine.at[t, j], dst, Z, z_devs[j // 2])

    needs_r = jnp.logical_not(col == y)
    gives_r = jnp.logical_not(other_col == y)

    def same(t, index, place, recv, peer):
        send(t, index, place, place, recv, peer)

    def transform(rows, dft_ref, traces_ref, mask_ref):
        per = NW // CHUNKS
        table = pltpu.make_async_copy(dft_hbm, dft_ref, inputs.at[CHUNKS])
        masks = pltpu.make_async_copy(mask_hbm, mask_ref, inputs.at[CHUNKS + 1])

        def chunk(i):
            part = pl.ds(i * per, per)
            return pltpu.make_async_copy(traces_hbm.at[part], traces_ref.at[part], inputs.at[i])

        table.start()
        masks.start()
        for i in range(CHUNKS):
            chunk(i).start()
        for peer in peers:
            pl.semaphore_signal(barrier, inc=1, device_id=peer, device_id_type=MESH)

        def whiten(w, spectrum):
            energy = jnp.sum(spectrum * spectrum, axis=0, keepdims=True) * (1.0 / SAMPLES)
            factor = mask_ref[pl.ds(w, 1), :].astype(jnp.float32) * lax.rsqrt(energy + EPSILON)
            rows[pl.ds(w, 2 * BINS, stride=NW), :] = spectrum * factor

        def one_chunk(i, carry):
            chunk(i).wait()
            for j in range(per // 2):
                w = i * per + 2 * j
                one, two = traces_ref[w], traces_ref[w + 1]
                spare = LANES - NS
                both = jnp.concatenate([one, two[:spare], two, one[:spare]], axis=0)
                spectrum = lax.dot_general(
                    dft_ref[...], both, NT_DIMS, preferred_element_type=jnp.float32
                )
                whiten(w, spectrum[:, :NS])
                whiten(w + 1, spectrum[:, LANES : LANES + NS])
            return carry

        table.wait()
        masks.wait()
        lax.fori_loop(0, CHUNKS, one_chunk, 0)
        pl.semaphore_wait(barrier, len(peers))

    def wait_only(ref, sem):
        pltpu.make_async_copy(ref, ref, sem).wait()

    r_slot = jnp.where(col == y, 0, 2)
    lane = lax.broadcasted_iota(jnp.int32, (1, LANES), 1)
    scale = 1.0 / math.sqrt(WINDOWS)

    def rows_of(t, slot, src):
        parts = [buf[t, slot + c % 2, c // 2, src // 4, src % 4] for c in range(4)]
        return jnp.concatenate(parts, axis=0)

    def fold(t, slot, pair, lo, split):
        tiles = []
        for src in (2 * pair, 2 * pair + 1):
            tile = rows_of(t, slot, src)
            if split:
                tile = jnp.where(lane >= lo + LANES, rows_of(t - 1, slot, src), tile)
            tiles.append(tile)
        return jnp.where(place(lo) < LANES // 2, tiles[0], pltpu.roll(tiles[1], LANES // 2, 1))

    def place(lo):
        return (lane - lo + LANES) % LANES

    def main(rows, lhs):
        def turn(t):
            for k in range(4):
                for i in range(2):
                    f = ((z + (0, 1, 3, 2)[k]) % 4) * 2 + (1 - xh if i else xh)
                    start = pl.multiple_of((f * NT + t) * LANES, LANES)
                    turned = rows[pl.ds(start, LANES), :].T.astype(jnp.bfloat16)
                    if k:
                        mine[t, 2 * (k - 1) + i] = turned
                    elif i:
                        wbuf[t, z] = turned
                    else:
                        buf[t, core, xl, xh, z] = turned
            z_sends(t)

        def one_bin(t, b, split):
            lo = 2 * NW * b - LANES * t
            half = place(lo) % (LANES // 2)
            for pair in range(4):
                tile = fold(t, 0, pair, lo, split)
                ahead = pltpu.roll(tile, LANES - NW, 1)
                back = pltpu.roll(tile, NW, 1)
                turned = jnp.where(half < NW, ahead, -back)
                zero = jnp.zeros_like(tile)
                part = pl.ds(pair * LANES, LANES)
                lhs[pl.ds(0, 4 * NS), part] = jnp.where(half < 2 * NW, tile, zero)
                lhs[pl.ds(4 * NS, 4 * NS), part] = jnp.where(half < 2 * NW, turned, zero)
            rhs = jnp.concatenate([fold(t, r_slot, pair, lo, split) for pair in range(4)], axis=1)
            product = lax.dot_general(
                lhs[...], rhs, NT_DIMS, preferred_element_type=jnp.float32
            )
            product = (product * scale).astype(jnp.bfloat16)
            out_ref[0, b] = product[: 4 * NS]
            out_ref[1, b] = product[4 * NS :]

        def multiply(t):
            first = (LANES * t) // (2 * NW)
            last = (LANES * (t + 1)) // (2 * NW)
            split = (t % PERIOD != 0).astype(jnp.int32)

            @pl.when(t % PERIOD != 0)
            def _():
                one_bin(t, first, True)

            def one(b, carry):
                one_bin(t, b, False)
                return carry

            lax.fori_loop(first + split, last, one, 0)

        def own(t):
            wait_only(mine.at[t], recvs.at[t, Z])
            send(t, 6, wbuf.at[t], piece(t, core, 4), X1, cross)
            same(t, 7, piece(t, core, 4), CA, twin)

        def own_s(t):
            own(t)
            send(t, 11, piece(t, core, 4), piece(t, slot_of(y), 4), O4, outer)

        def own_t(t):
            own(t)
            send(t, 11, wbuf.at[t], free(t, outer_y, 0), O4, outer)

        def near(t):
            wait_only(piece(t, core, 3), recvs.at[t, X1])
            same(t, 8, piece(t, core, 3), CB, twin)

        def near_s(t):
            near(t)
            send(t, 12, piece(t, core, 3), piece(t, slot_of(y), 3), P2, pair)

        def twin_a(t):
            wait_only(piece(t, core, 1), recvs.at[t, CA])

        def twin_a_s(t):
            twin_a(t)
            send(t, 13, piece(t, core, 1), piece(t, slot_of(y), 1), O1, outer)

        def whole(t):
            wait_only(piece(t, core, 2), recvs.at[t, CB])

        def whole_s(t):
            whole(t)
            send(t, 15, piece(t, core, 2), piece(t, slot_of(y), 2), O2, outer)
            send(t, 14, piece(t, core, 2), piece(t, slot_of(y), 2), P2, pair)
            same(t, 9, buf.at[t, core], CL, mate)

        def whole_t(t):
            whole(t)
            same(t, 9, buf.at[t, core], CL, mate)

        def relay(t, index, k, recv, recv_next):
            held = piece(t, slot_of(outer_y), k)
            wait_only(held, recvs.at[t, recv])
            same(t, index, held, recv_next, pair)

        def relay_4(t):
            relay(t, 12, 4, O4, P4)

        def relay_1(t):
            relay(t, 13, 1, O1, P1)

        def relay_2(t):
            relay(t, 14, 2, O2, P2)

        def next_outer(t):
            held = free(t, y, 0)
            wait_only(held, recvs.at[t, O4])
            send(t, 16, held, free(t, pair_y, 1), P4, pair)
            send(t, 17, held, buf.at[t, slot_of(outer_y, x_col), xl, xh], XW, cross)

        def next_far(t):
            held = free(t, y, 1)
            wait_only(held, recvs.at[t, P4])
            send(t, 18, held, buf.at[t, slot_of(far_y, x_col), xl, xh], XW, cross)

        def loop(t, index, k, recv):
            held = piece(t, slot_of(far_y), k)
            wait_only(held, recvs.at[t, recv])
            same(t, index, held, O1, outer)

        def loop_4(t):
            loop(t, 15, 4, P4)

        def loop_1(t):
            loop(t, 16, 1, P1)

        def give(t):
            @pl.when(gives_r)
            def _():
                send(t, 10, buf.at[t, 4], buf.at[t, 2 + core], CR, mate)

        def rows_s(t):
            wait_only(buf.at[t, 4, xl], recvs.at[t, P2])
            wait_only(buf.at[t, 4, xl], recvs.at[t, O1])
            give(t)

        def rows_t(t):
            wait_only(piece(t, slot_of(far_y), 2), recvs.at[t, P2])
            wait_only(buf.at[t, 4, xl], recvs.at[t, XW])
            give(t)

        def products(t):
            wait_only(buf.at[t, 1 - core], recvs.at[t, CL])

            @pl.when(needs_r)
            def _():
                wait_only(buf.at[t, 3 - core], recvs.at[t, CR])

            multiply(t)

        events = {
            "turn": turn, "products": products,
            "own_s": own_s, "near_s": near_s, "twin_a_s": twin_a_s, "whole_s": whole_s,
            "next_outer": next_outer, "next_far": next_far, "rows_s": rows_s,
            "own_t": own_t, "near_t": near, "twin_a_t": twin_a, "whole_t": whole_t,
            "relay_4": relay_4, "relay_1": relay_1, "relay_2": relay_2,
            "loop_4": loop_4, "loop_1": loop_1, "rows_t": rows_t,
        }

        def step(tau, carry):
            for who, name, lag in ORDER:
                run = jnp.logical_and(tau >= lag, tau < NT + lag)
                if who != "B":
                    run = jnp.logical_and(run, is_source if who == "S" else is_relay)

                @pl.when(run)
                def _():
                    events[name](tau - lag)

            return carry

        lags = {name: lag for _, name, lag in ORDER}
        for t in range(-lags["turn"]):
            turn(t)
        lax.fori_loop(0, NT + max(lags.values()), step, 0)

    def stages(rows):
        pl.run_scoped(
            functools.partial(transform, rows),
            pltpu.VMEM((2 * BINS, SAMPLES), jnp.bfloat16),
            pltpu.VMEM((NW, NS, SAMPLES), jnp.bfloat16),
            pltpu.VMEM((NW, NS), jnp.int32),
        )
        pl.run_scoped(
            lambda lhs: main(rows, lhs), pltpu.VMEM((8 * NS, 4 * LANES), jnp.bfloat16)
        )

    pl.run_scoped(stages, pltpu.VMEM((2 * BINS * NW, NS), jnp.float32))

    one, two = wbuf, buf.at[:, core]
    for j in range(6):
        wait_only(mine.at[:, j], sends.at[j])
    for j in (6, 7, 8, 11, 12, 13, 14, 15, 16):
        wait_only(one, sends.at[j])
    wait_only(two, sends.at[9])

    @pl.when(gives_r)
    def _():
        wait_only(two, sends.at[10])

    @pl.when(is_source)
    def _():
        for j in (17, 18):
            wait_only(one, sends.at[j])


def hbm(array):
    return pltpu.with_memory_space_constraint(array, pltpu.HBM)


def shards(traces, window_mask):
    dft = jnp.asarray(dft_table().astype(jnp.bfloat16))
    dma = pltpu.SemaphoreType.DMA
    bf16 = jnp.bfloat16
    return pl.pallas_call(
        kernel,
        out_shape=jax.ShapeDtypeStruct((2, 32, 320, 320), bf16),
        in_specs=[pl.BlockSpec(memory_space=pltpu.HBM)] * 3,
        out_specs=pl.BlockSpec(memory_space=pltpu.VMEM),
        scratch_shapes=[
            pltpu.VMEM((NT, 6, NS, LANES), bf16),
            pltpu.VMEM((NT, 4, NS, LANES), bf16),
            pltpu.VMEM((NT, 5, 2, 2, 4, NS, LANES), bf16),
            dma((CHUNKS + 2,)), dma((19,)), dma((NT, 13)),
        ],
        compiler_params=pltpu.CompilerParams(
            collective_id=0, has_side_effects=True, vmem_limit_bytes=36 * 2**20
        ),
        cost_estimate=pl.CostEstimate(
            flops=12 * 10**9, bytes_accessed=20 * 10**6, transcendentals=0
        ),
        name="cross_spectra",
    )(hbm(dft), hbm(jnp.transpose(traces, (1, 0, 2))), hbm(jnp.transpose(window_mask)))


def solution(mesh):
    placed = (P(("row", "col"), "freq", None), P(("row", "col"), "freq"))
    return jax.shard_map(
        shards, mesh=mesh, in_specs=placed, out_specs=P(None, "freq", "row", "col"), check_vma=False
    )
```

```python
import functools
import math

import jax
import jax.numpy as jnp
import numpy as np
from jax import lax
from jax.experimental import pallas as pl
from jax.experimental.pallas import tpu as pltpu
from jax.sharding import PartitionSpec as P

SAMPLES = 512
BINS = 256
EPSILON = 1e-06
NS = 80
NW = 28
LANES = 128
NT = 14
PERIOD = 7
RING = 8
CHUNKS = 2
WINDOWS = 224
MESH = pl.DeviceIdType.MESH
NT_DIMS = (((1,), (1,)), ((), ()))

ORDER = (
    ("T", "own_t", 0),
    ("S", "next_outer", 2),
    ("S", "whole_s", 3),
    ("T", "relay_4", 1),
    ("T", "near_t", 1),
    ("B", "products", 6),
    ("T", "relay_1", 2),
    ("T", "loop_1", 3),
    ("B", "turn", -2),
    ("T", "loop_4", 2),
    ("S", "near_s", 2),
    ("T", "twin_a_t", 1),
    ("T", "whole_t", 3),
    ("T", "relay_2", 3),
    ("S", "own_s", 0),
    ("S", "twin_a_s", 1),
    ("S", "next_far", 3),
    ("T", "rows_t", 4),
    ("S", "rows_s", 4),
)
Z, X1, CA, CB, CL, CR, O4, O1, O2, P4, P1, P2, XW = range(13)


def dft_table():
    t = np.arange(SAMPLES, dtype=np.int64)
    k = np.arange(BINS, dtype=np.int64)
    angles = 2.0 * math.pi / SAMPLES * ((k[:, None] * t[None, :]) % SAMPLES)
    taper = 0.5 - 0.5 * np.cos(2.0 * math.pi / SAMPLES * t)
    stacked = np.stack([taper * np.cos(angles), -taper * np.sin(angles)], axis=1)
    return stacked.reshape(2 * BINS, SAMPLES).astype(np.float32)


def kernel(
    dft_hbm, traces_hbm, mask_hbm, out_ref, mine, wbuf, buf, inputs, sends, recvs,
):
    y = lax.axis_index("row")
    col = lax.axis_index("col")
    freq = lax.axis_index("freq")
    xl, core = col // 2, col % 2
    z, xh = freq // 2, freq % 2
    pair_y = y + 1 - 2 * (y % 2)
    outer_y = 3 - y
    far_y = 3 - pair_y
    is_source = (y // 2) == xl
    is_relay = jnp.logical_not(is_source)
    other_col = col + 1 - 2 * core
    x_col = (1 - xl) * 2 + core
    x_freq = z * 2 + 1 - xh

    others = [((z + k) % 4) for k in (1, 3, 2)]
    z_devs = [(y, col, o * 2 + xh) for o in others]
    twin = (y, x_col, freq)
    cross = (y, x_col, x_freq)
    pair = (pair_y, col, freq)
    outer = (outer_y, col, freq)
    mate = (y, other_col, freq)

    barrier = pltpu.get_barrier_semaphore()
    peers = z_devs + [twin, cross, pair, outer, mate]

    def remote(src, dst, send, recv, peer):
        return pltpu.make_async_remote_copy(
            src_ref=src, dst_ref=dst, send_sem=send, recv_sem=recv,
            device_id=peer, device_id_type=MESH,
        )

    def slot_of(row_, col_=col):
        return jnp.where(row_ == col_, 2 + core, 4)

    def free(t, row_, i):
        return buf.at[t, jnp.where(row_ == col, 2, 4), 0, i]

    def piece(t, slot, k):
        a, b = {1: (1 - xl, xh), 2: (xl, 1 - xh), 3: (1 - xl, 1 - xh), 4: (xl, xh)}[k]
        return buf.at[t, slot, a, b]

    def send(t, index, src, dst, recv, peer):
        return remote(src, dst, sends.at[index], recvs.at[t % RING, recv], peer).start()

    def z_sends(t):
        for j in range(6):
            dst = wbuf.at[t, z] if j % 2 else buf.at[t, core, xl, xh, z]
            send(t, j, mine.at[t, j], dst, Z, z_devs[j // 2])

    needs_r = jnp.logical_not(col == y)
    gives_r = jnp.logical_not(other_col == y)

    def same(t, index, place, recv, peer):
        send(t, index, place, place, recv, peer)

    def transform(rows, dft_ref, traces_ref, mask_ref):
        per = NW // CHUNKS
        table = pltpu.make_async_copy(dft_hbm, dft_ref, inputs.at[CHUNKS])
        masks = pltpu.make_async_copy(mask_hbm, mask_ref, inputs.at[CHUNKS + 1])

        def chunk(i):
            part = pl.ds(i * per, per)
            return pltpu.make_async_copy(traces_hbm.at[part], traces_ref.at[part], inputs.at[i])

        table.start()
        masks.start()
        for i in range(CHUNKS):
            chunk(i).start()
        for peer in peers:
            pl.semaphore_signal(barrier, inc=1, device_id=peer, device_id_type=MESH)

        def whiten(w, spectrum):
            energy = jnp.sum(spectrum * spectrum, axis=0, keepdims=True) * (1.0 / SAMPLES)
            factor = mask_ref[pl.ds(w, 1), :].astype(jnp.float32) * lax.rsqrt(energy + EPSILON)
            rows[pl.ds(w, 2 * BINS, stride=NW), :] = spectrum * factor

        def one_chunk(i, carry):
            chunk(i).wait()
            for j in range(per // 2):
                w = i * per + 2 * j
                one, two = traces_ref[w], traces_ref[w + 1]
                spare = LANES - NS
                both = jnp.concatenate([one, two[:spare], two, one[:spare]], axis=0)
                spectrum = lax.dot_general(
                    dft_ref[...], both, NT_DIMS, preferred_element_type=jnp.float32
                )
                whiten(w, spectrum[:, :NS])
                whiten(w + 1, spectrum[:, LANES : LANES + NS])
            return carry

        table.wait()
        masks.wait()
        lax.fori_loop(0, CHUNKS, one_chunk, 0)
        pl.semaphore_wait(barrier, len(peers))

    def wait_only(ref, sem):
        pltpu.make_async_copy(ref, ref, sem).wait()

    r_slot = jnp.where(col == y, 0, 2)
    lane = lax.broadcasted_iota(jnp.int32, (1, LANES), 1)
    scale = 1.0 / math.sqrt(WINDOWS)

    def rows_of(t, slot, src):
        parts = [buf[t, slot + c % 2, c // 2, src // 4, src % 4] for c in range(4)]
        return jnp.concatenate(parts, axis=0)

    def fold(t, slot, pair, lo, split):
        tiles = []
        for src in (2 * pair, 2 * pair + 1):
            tile = rows_of(t, slot, src)
            if split:
                tile = jnp.where(lane >= lo + LANES, rows_of(t - 1, slot, src), tile)
            tiles.append(tile)
        return jnp.where(place(lo) < LANES // 2, tiles[0], pltpu.roll(tiles[1], LANES // 2, 1))

    def place(lo):
        return (lane - lo + LANES) % LANES

    def main(rows, lhs):
        def turn(t):
            for k in range(4):
                for i in range(2):
                    f = ((z + (0, 1, 3, 2)[k]) % 4) * 2 + (1 - xh if i else xh)
                    start = pl.multiple_of((f * NT + t) * LANES, LANES)
                    turned = rows[pl.ds(start, LANES), :].T.astype(jnp.bfloat16)
                    if k:
                        mine[t, 2 * (k - 1) + i] = turned
                    elif i:
                        wbuf[t, z] = turned
                    else:
                        buf[t, core, xl, xh, z] = turned
            z_sends(t)

        def one_bin(t, b, split):
            lo = 2 * NW * b - LANES * t
            half = place(lo) % (LANES // 2)
            for pair in range(4):
                tile = fold(t, 0, pair, lo, split)
                ahead = pltpu.roll(tile, LANES - NW, 1)
                back = pltpu.roll(tile, NW, 1)
                turned = jnp.where(half < NW, ahead, -back)
                zero = jnp.zeros_like(tile)
                part = pl.ds(pair * LANES, LANES)
                lhs[pl.ds(0, 4 * NS), part] = jnp.where(half < 2 * NW, tile, zero)
                lhs[pl.ds(4 * NS, 4 * NS), part] = jnp.where(half < 2 * NW, turned, zero)
            rhs = jnp.concatenate([fold(t, r_slot, pair, lo, split) for pair in range(4)], axis=1)
            product = lax.dot_general(
                lhs[...], rhs, NT_DIMS, preferred_element_type=jnp.float32
            )
            product = (product * scale).astype(jnp.bfloat16)
            out_ref[0, b] = product[: 4 * NS]
            out_ref[1, b] = product[4 * NS :]

        def multiply(t):
            first = (LANES * t) // (2 * NW)
            last = (LANES * (t + 1)) // (2 * NW)
            split = (t % PERIOD != 0).astype(jnp.int32)

            @pl.when(t % PERIOD != 0)
            def _():
                one_bin(t, first, True)

            def one(b, carry):
                one_bin(t, b, False)
                return carry

            lax.fori_loop(first + split, last, one, 0)

        def own(t):
            wait_only(mine.at[t], recvs.at[t % RING, Z])
            send(t, 6, wbuf.at[t], piece(t, core, 4), X1, cross)
            same(t, 7, piece(t, core, 4), CA, twin)

        def own_s(t):
            own(t)
            send(t, 11, piece(t, core, 4), piece(t, slot_of(y), 4), O4, outer)

        def own_t(t):
            own(t)
            send(t, 11, wbuf.at[t], free(t, outer_y, 0), O4, outer)

        def near(t):
            wait_only(piece(t, core, 3), recvs.at[t % RING, X1])
            same(t, 8, piece(t, core, 3), CB, twin)

        def near_s(t):
            near(t)
            send(t, 12, piece(t, core, 3), piece(t, slot_of(y), 3), P2, pair)

        def twin_a(t):
            wait_only(piece(t, core, 1), recvs.at[t % RING, CA])

        def twin_a_s(t):
            twin_a(t)
            send(t, 13, piece(t, core, 1), piece(t, slot_of(y), 1), O1, outer)

        def whole(t):
            wait_only(piece(t, core, 2), recvs.at[t % RING, CB])

        def whole_s(t):
            whole(t)
            send(t, 15, piece(t, core, 2), piece(t, slot_of(y), 2), O2, outer)
            send(t, 14, piece(t, core, 2), piece(t, slot_of(y), 2), P2, pair)
            same(t, 9, buf.at[t, core], CL, mate)

        def whole_t(t):
            whole(t)
            same(t, 9, buf.at[t, core], CL, mate)

        def relay(t, index, k, recv, recv_next):
            held = piece(t, slot_of(outer_y), k)
            wait_only(held, recvs.at[t % RING, recv])
            same(t, index, held, recv_next, pair)

        def relay_4(t):
            relay(t, 12, 4, O4, P4)

        def relay_1(t):
            relay(t, 13, 1, O1, P1)

        def relay_2(t):
            relay(t, 14, 2, O2, P2)

        def next_outer(t):
            held = free(t, y, 0)
            wait_only(held, recvs.at[t % RING, O4])
            send(t, 16, held, free(t, pair_y, 1), P4, pair)
            send(t, 17, held, buf.at[t, slot_of(outer_y, x_col), xl, xh], XW, cross)

        def next_far(t):
            held = free(t, y, 1)
            wait_only(held, recvs.at[t % RING, P4])
            send(t, 18, held, buf.at[t, slot_of(far_y, x_col), xl, xh], XW, cross)

        def loop(t, index, k, recv):
            held = piece(t, slot_of(far_y), k)
            wait_only(held, recvs.at[t % RING, recv])
            same(t, index, held, O1, outer)

        def loop_4(t):
            loop(t, 15, 4, P4)

        def loop_1(t):
            loop(t, 16, 1, P1)

        def give(t):
            @pl.when(gives_r)
            def _():
                send(t, 10, buf.at[t, 4], buf.at[t, 2 + core], CR, mate)

        def rows_s(t):
            wait_only(buf.at[t, 4, xl], recvs.at[t % RING, P2])
            wait_only(buf.at[t, 4, xl], recvs.at[t % RING, O1])
            give(t)

        def rows_t(t):
            wait_only(piece(t, slot_of(far_y), 2), recvs.at[t % RING, P2])
            wait_only(buf.at[t, 4, xl], recvs.at[t % RING, XW])
            give(t)

        def products(t):
            wait_only(buf.at[t, 1 - core], recvs.at[t % RING, CL])

            @pl.when(needs_r)
            def _():
                wait_only(buf.at[t, 3 - core], recvs.at[t % RING, CR])

            multiply(t)

        events = {
            "turn": turn, "products": products,
            "own_s": own_s, "near_s": near_s, "twin_a_s": twin_a_s, "whole_s": whole_s,
            "next_outer": next_outer, "next_far": next_far, "rows_s": rows_s,
            "own_t": own_t, "near_t": near, "twin_a_t": twin_a, "whole_t": whole_t,
            "relay_4": relay_4, "relay_1": relay_1, "relay_2": relay_2,
            "loop_4": loop_4, "loop_1": loop_1, "rows_t": rows_t,
        }

        def step(tau, carry):
            for who, name, lag in ORDER:
                run = jnp.logical_and(tau >= lag, tau < NT + lag)
                if who != "B":
                    run = jnp.logical_and(run, is_source if who == "S" else is_relay)

                @pl.when(run)
                def _():
                    events[name](tau - lag)

            return carry

        lags = {name: lag for _, name, lag in ORDER}
        for t in range(-lags["turn"]):
            turn(t)
        lax.fori_loop(0, NT + max(lags.values()), step, 0)

    def stages(rows):
        pl.run_scoped(
            functools.partial(transform, rows),
            pltpu.VMEM((2 * BINS, SAMPLES), jnp.bfloat16),
            pltpu.VMEM((NW, NS, SAMPLES), jnp.bfloat16),
            pltpu.VMEM((NW, NS), jnp.int32),
        )
        pl.run_scoped(
            lambda lhs: main(rows, lhs), pltpu.VMEM((8 * NS, 4 * LANES), jnp.bfloat16)
        )

    pl.run_scoped(stages, pltpu.VMEM((2 * BINS * NW, NS), jnp.float32))

    one, two = wbuf, buf.at[:, core]
    for j in range(6):
        wait_only(mine.at[:, j], sends.at[j])
    for j in (6, 7, 8, 11, 12, 13, 14, 15, 16):
        wait_only(one, sends.at[j])
    wait_only(two, sends.at[9])

    @pl.when(gives_r)
    def _():
        wait_only(two, sends.at[10])

    @pl.when(is_source)
    def _():
        for j in (17, 18):
            wait_only(one, sends.at[j])


def hbm(array):
    return pltpu.with_memory_space_constraint(array, pltpu.HBM)


def shards(traces, window_mask):
    dft = jnp.asarray(dft_table().astype(jnp.bfloat16))
    dma = pltpu.SemaphoreType.DMA
    bf16 = jnp.bfloat16
    return pl.pallas_call(
        kernel,
        out_shape=jax.ShapeDtypeStruct((2, 32, 320, 320), bf16),
        in_specs=[pl.BlockSpec(memory_space=pltpu.HBM)] * 3,
        out_specs=pl.BlockSpec(memory_space=pltpu.VMEM),
        scratch_shapes=[
            pltpu.VMEM((NT, 6, NS, LANES), bf16),
            pltpu.VMEM((NT, 4, NS, LANES), bf16),
            pltpu.VMEM((NT, 5, 2, 2, 4, NS, LANES), bf16),
            dma((CHUNKS + 2,)), dma((19,)), dma((RING, 13)),
        ],
        compiler_params=pltpu.CompilerParams(
            collective_id=0, has_side_effects=True, vmem_limit_bytes=36 * 2**20
        ),
        cost_estimate=pl.CostEstimate(
            flops=12 * 10**9, bytes_accessed=20 * 10**6, transcendentals=0
        ),
        name="cross_spectra",
    )(hbm(dft), hbm(jnp.transpose(traces, (1, 0, 2))), hbm(jnp.transpose(window_mask)))


def solution(mesh):
    placed = (P(("row", "col"), "freq", None), P(("row", "col"), "freq"))
    return jax.shard_map(
        shards, mesh=mesh, in_specs=placed, out_specs=P(None, "freq", "row", "col"), check_vma=False
    )
```

```python
import functools
import math

import jax
import jax.numpy as jnp
import numpy as np
from jax import lax
from jax.experimental import pallas as pl
from jax.experimental.pallas import tpu as pltpu
from jax.sharding import PartitionSpec as P

SAMPLES = 512
BINS = 256
EPSILON = 1e-06
NS = 80
NW = 28
LANES = 128
NT = 14
PERIOD = 7
TAIL = 2
BEGUN = LANES * (NT - TAIL) // (2 * NW)
PARTS = 3
RING = 8
CHUNKS = 2
WINDOWS = 224
MESH = pl.DeviceIdType.MESH
NT_DIMS = (((1,), (1,)), ((), ()))

ORDER = (
    ("T", "own_t", 0),
    ("S", "next_outer", 2),
    ("S", "whole_s", 3),
    ("T", "relay_4", 1),
    ("T", "near_t", 1),
    ("B", "products", 6),
    ("T", "relay_1", 2),
    ("T", "loop_1", 3),
    ("B", "turn", -2),
    ("T", "loop_4", 2),
    ("S", "near_s", 2),
    ("T", "twin_a_t", 1),
    ("T", "whole_t", 3),
    ("T", "relay_2", 3),
    ("S", "own_s", 0),
    ("S", "twin_a_s", 1),
    ("S", "next_far", 3),
    ("T", "rows_t", 4),
    ("S", "rows_s", 4),
)
Z, X1, CA, CB, CL, CR, O4, O1, O2, P4, P1, P2, XW = range(13)


def dft_table():
    t = np.arange(SAMPLES, dtype=np.int64)
    k = np.arange(BINS, dtype=np.int64)
    angles = 2.0 * math.pi / SAMPLES * ((k[:, None] * t[None, :]) % SAMPLES)
    taper = 0.5 - 0.5 * np.cos(2.0 * math.pi / SAMPLES * t)
    stacked = np.stack([taper * np.cos(angles), -taper * np.sin(angles)], axis=1)
    return stacked.reshape(2 * BINS, SAMPLES).astype(np.float32)


def products_of(buf, lhs, r_slot, put):
    lane = lax.broadcasted_iota(jnp.int32, (1, LANES), 1)
    scale = 1.0 / math.sqrt(WINDOWS)

    def rows_of(t, slot, src):
        parts = [buf[t, slot + c % 2, c // 2, src // 4, src % 4] for c in range(4)]
        return jnp.concatenate(parts, axis=0)

    def fold(t, slot, pair, lo, split):
        tiles = []
        for src in (2 * pair, 2 * pair + 1):
            tile = rows_of(t, slot, src)
            if split:
                tile = jnp.where(lane >= lo + LANES, rows_of(t - 1, slot, src), tile)
            tiles.append(tile)
        return jnp.where(place(lo) < LANES // 2, tiles[0], pltpu.roll(tiles[1], LANES // 2, 1))

    def place(lo):
        return (lane - lo + LANES) % LANES

    def one_bin(t, b, split):
        lo = 2 * NW * b - LANES * t
        half = place(lo) % (LANES // 2)
        for pair in range(4):
            tile = fold(t, 0, pair, lo, split)
            ahead = pltpu.roll(tile, LANES - NW, 1)
            back = pltpu.roll(tile, NW, 1)
            turned = jnp.where(half < NW, ahead, -back)
            zero = jnp.zeros_like(tile)
            part = pl.ds(pair * LANES, LANES)
            lhs[pl.ds(0, 4 * NS), part] = jnp.where(half < 2 * NW, tile, zero)
            lhs[pl.ds(4 * NS, 4 * NS), part] = jnp.where(half < 2 * NW, turned, zero)
        rhs = jnp.concatenate([fold(t, r_slot, pair, lo, split) for pair in range(4)], axis=1)
        product = lax.dot_general(
            lhs[...], rhs, NT_DIMS, preferred_element_type=jnp.float32
        )
        product = (product * scale).astype(jnp.bfloat16)
        put(b, product[: 4 * NS], product[4 * NS :])

    def multiply(t):
        first = (LANES * t) // (2 * NW)
        last = (LANES * (t + 1)) // (2 * NW)
        split = (t % PERIOD != 0).astype(jnp.int32)

        @pl.when(t % PERIOD != 0)
        def _():
            one_bin(t, first, True)

        def one(b, carry):
            one_bin(t, b, False)
            return carry

        lax.fori_loop(first + split, last, one, 0)

    return multiply


def kernel(
    dft_hbm, traces_hbm, mask_hbm, out_ref, buf, mine, wbuf, inputs, sends, recvs,
):
    y = lax.axis_index("row")
    col = lax.axis_index("col")
    freq = lax.axis_index("freq")
    xl, core = col // 2, col % 2
    z, xh = freq // 2, freq % 2
    pair_y = y + 1 - 2 * (y % 2)
    outer_y = 3 - y
    far_y = 3 - pair_y
    is_source = (y // 2) == xl
    is_relay = jnp.logical_not(is_source)
    other_col = col + 1 - 2 * core
    x_col = (1 - xl) * 2 + core
    x_freq = z * 2 + 1 - xh

    others = [((z + k) % 4) for k in (1, 3, 2)]
    z_devs = [(y, col, o * 2 + xh) for o in others]
    twin = (y, x_col, freq)
    cross = (y, x_col, x_freq)
    pair = (pair_y, col, freq)
    outer = (outer_y, col, freq)
    mate = (y, other_col, freq)

    barrier = pltpu.get_barrier_semaphore()
    peers = z_devs + [twin, cross, pair, outer, mate]

    def remote(src, dst, send, recv, peer):
        return pltpu.make_async_remote_copy(
            src_ref=src, dst_ref=dst, send_sem=send, recv_sem=recv,
            device_id=peer, device_id_type=MESH,
        )

    def slot_of(row_, col_=col):
        return jnp.where(row_ == col_, 2 + core, 4)

    def free(t, row_, i):
        return buf.at[t, jnp.where(row_ == col, 2, 4), 0, i]

    def piece(t, slot, k):
        a, b = {1: (1 - xl, xh), 2: (xl, 1 - xh), 3: (1 - xl, 1 - xh), 4: (xl, xh)}[k]
        return buf.at[t, slot, a, b]

    def send(t, index, src, dst, recv, peer):
        return remote(src, dst, sends.at[index], recvs.at[t % RING, recv], peer).start()

    def z_sends(t):
        for j in range(6):
            dst = wbuf.at[t, z] if j % 2 else buf.at[t, core, xl, xh, z]
            send(t, j, mine.at[t, j], dst, Z, z_devs[j // 2])

    needs_r = jnp.logical_not(col == y)
    gives_r = jnp.logical_not(other_col == y)

    def same(t, index, place, recv, peer):
        send(t, index, place, place, recv, peer)

    def transform(rows, dft_ref, traces_ref, mask_ref):
        per = NW // CHUNKS
        table = pltpu.make_async_copy(dft_hbm, dft_ref, inputs.at[CHUNKS])
        masks = pltpu.make_async_copy(mask_hbm, mask_ref, inputs.at[CHUNKS + 1])

        def chunk(i):
            part = pl.ds(i * per, per)
            return pltpu.make_async_copy(traces_hbm.at[part], traces_ref.at[part], inputs.at[i])

        table.start()
        masks.start()
        for i in range(CHUNKS):
            chunk(i).start()
        for peer in peers:
            pl.semaphore_signal(barrier, inc=1, device_id=peer, device_id_type=MESH)

        def whiten(w, spectrum):
            energy = jnp.sum(spectrum * spectrum, axis=0, keepdims=True) * (1.0 / SAMPLES)
            factor = mask_ref[pl.ds(w, 1), :].astype(jnp.float32) * lax.rsqrt(energy + EPSILON)
            rows[pl.ds(w, 2 * BINS, stride=NW), :] = spectrum * factor

        def one_chunk(i, carry):
            chunk(i).wait()
            for j in range(per // 2):
                w = i * per + 2 * j
                one, two = traces_ref[w], traces_ref[w + 1]
                spare = LANES - NS
                both = jnp.concatenate([one, two[:spare], two, one[:spare]], axis=0)
                spectrum = lax.dot_general(
                    dft_ref[...], both, NT_DIMS, preferred_element_type=jnp.float32
                )
                whiten(w, spectrum[:, :NS])
                whiten(w + 1, spectrum[:, LANES : LANES + NS])
            return carry

        table.wait()
        masks.wait()
        lax.fori_loop(0, CHUNKS, one_chunk, 0)
        pl.semaphore_wait(barrier, len(peers))

    def wait_only(ref, sem):
        pltpu.make_async_copy(ref, ref, sem).wait()

    def main(rows, lhs):
        def turn(t):
            for k in range(4):
                for i in range(2):
                    f = ((z + (0, 1, 3, 2)[k]) % 4) * 2 + (1 - xh if i else xh)
                    start = pl.multiple_of((f * NT + t) * LANES, LANES)
                    turned = rows[pl.ds(start, LANES), :].T.astype(jnp.bfloat16)
                    if k:
                        mine[t, 2 * (k - 1) + i] = turned
                    elif i:
                        wbuf[t, z] = turned
                    else:
                        buf[t, core, xl, xh, z] = turned
            z_sends(t)

        def put(b, real, imag):
            out_ref[0, b] = real
            out_ref[1, b] = imag

        multiply = products_of(buf, lhs, jnp.where(col == y, 0, 2), put)

        def own(t):
            wait_only(mine.at[t], recvs.at[t % RING, Z])
            send(t, 6, wbuf.at[t], piece(t, core, 4), X1, cross)
            same(t, 7, piece(t, core, 4), CA, twin)

        def own_s(t):
            own(t)
            send(t, 11, piece(t, core, 4), piece(t, slot_of(y), 4), O4, outer)

        def own_t(t):
            own(t)
            send(t, 11, wbuf.at[t], free(t, outer_y, 0), O4, outer)

        def near(t):
            wait_only(piece(t, core, 3), recvs.at[t % RING, X1])
            same(t, 8, piece(t, core, 3), CB, twin)

        def near_s(t):
            near(t)
            send(t, 12, piece(t, core, 3), piece(t, slot_of(y), 3), P2, pair)

        def twin_a(t):
            wait_only(piece(t, core, 1), recvs.at[t % RING, CA])

        def twin_a_s(t):
            twin_a(t)
            send(t, 13, piece(t, core, 1), piece(t, slot_of(y), 1), O1, outer)

        def whole(t):
            wait_only(piece(t, core, 2), recvs.at[t % RING, CB])

        def whole_s(t):
            whole(t)
            send(t, 15, piece(t, core, 2), piece(t, slot_of(y), 2), O2, outer)
            send(t, 14, piece(t, core, 2), piece(t, slot_of(y), 2), P2, pair)
            same(t, 9, buf.at[t, core], CL, mate)

        def whole_t(t):
            whole(t)
            same(t, 9, buf.at[t, core], CL, mate)

        def relay(t, index, k, recv, recv_next):
            held = piece(t, slot_of(outer_y), k)
            wait_only(held, recvs.at[t % RING, recv])
            same(t, index, held, recv_next, pair)

        def relay_4(t):
            relay(t, 12, 4, O4, P4)

        def relay_1(t):
            relay(t, 13, 1, O1, P1)

        def relay_2(t):
            relay(t, 14, 2, O2, P2)

        def next_outer(t):
            held = free(t, y, 0)
            wait_only(held, recvs.at[t % RING, O4])
            send(t, 16, held, free(t, pair_y, 1), P4, pair)
            send(t, 17, held, buf.at[t, slot_of(outer_y, x_col), xl, xh], XW, cross)

        def next_far(t):
            held = free(t, y, 1)
            wait_only(held, recvs.at[t % RING, P4])
            send(t, 18, held, buf.at[t, slot_of(far_y, x_col), xl, xh], XW, cross)

        def loop(t, index, k, recv):
            held = piece(t, slot_of(far_y), k)
            wait_only(held, recvs.at[t % RING, recv])
            same(t, index, held, O1, outer)

        def loop_4(t):
            loop(t, 15, 4, P4)

        def loop_1(t):
            loop(t, 16, 1, P1)

        def give(t):
            @pl.when(gives_r)
            def _():
                send(t, 10, buf.at[t, 4], buf.at[t, 2 + core], CR, mate)

        def rows_s(t):
            wait_only(buf.at[t, 4, xl], recvs.at[t % RING, P2])
            wait_only(buf.at[t, 4, xl], recvs.at[t % RING, O1])
            give(t)

        def rows_t(t):
            wait_only(piece(t, slot_of(far_y), 2), recvs.at[t % RING, P2])
            wait_only(buf.at[t, 4, xl], recvs.at[t % RING, XW])
            give(t)

        def products(t):
            wait_only(buf.at[t, 1 - core], recvs.at[t % RING, CL])

            @pl.when(needs_r)
            def _():
                wait_only(buf.at[t, 3 - core], recvs.at[t % RING, CR])

            @pl.when(t < NT - TAIL)
            def _():
                multiply(t)

        events = {
            "turn": turn, "products": products,
            "own_s": own_s, "near_s": near_s, "twin_a_s": twin_a_s, "whole_s": whole_s,
            "next_outer": next_outer, "next_far": next_far, "rows_s": rows_s,
            "own_t": own_t, "near_t": near, "twin_a_t": twin_a, "whole_t": whole_t,
            "relay_4": relay_4, "relay_1": relay_1, "relay_2": relay_2,
            "loop_4": loop_4, "loop_1": loop_1, "rows_t": rows_t,
        }

        def step(tau, carry):
            for who, name, lag in ORDER:
                run = jnp.logical_and(tau >= lag, tau < NT + lag)
                if who != "B":
                    run = jnp.logical_and(run, is_source if who == "S" else is_relay)

                @pl.when(run)
                def _():
                    events[name](tau - lag)

            return carry

        lags = {name: lag for _, name, lag in ORDER}
        for t in range(-lags["turn"]):
            turn(t)
        lax.fori_loop(0, NT + max(lags.values()), step, 0)

    def stages(rows):
        pl.run_scoped(
            functools.partial(transform, rows),
            pltpu.VMEM((2 * BINS, SAMPLES), jnp.bfloat16),
            pltpu.VMEM((NW, NS, SAMPLES), jnp.bfloat16),
            pltpu.VMEM((NW, NS), jnp.int32),
        )
        pl.run_scoped(
            lambda lhs: main(rows, lhs), pltpu.VMEM((8 * NS, 4 * LANES), jnp.bfloat16)
        )

    pl.run_scoped(stages, pltpu.VMEM((2 * BINS * NW, NS), jnp.float32))

    one, two = wbuf, buf.at[:, core]
    for j in range(6):
        wait_only(mine.at[:, j], sends.at[j])
    for j in (6, 7, 8, 11, 12, 13, 14, 15, 16):
        wait_only(one, sends.at[j])
    wait_only(two, sends.at[9])

    @pl.when(gives_r)
    def _():
        wait_only(two, sends.at[10])

    @pl.when(is_source)
    def _():
        for j in (17, 18):
            wait_only(one, sends.at[j])


def finish_kernel(begun, buf, out_hbm, lhs, last, sems):
    per = BEGUN // PARTS
    copies = []
    for c in range(2):
        for i in range(PARTS):
            part = pl.ds(i * per, per)
            copies.append(
                pltpu.make_async_copy(begun.at[c, part], out_hbm.at[c, part], sems.at[c, i])
            )
    for copy in copies:
        copy.start()

    def put(b, real, imag):
        last[0, b - BEGUN] = real
        last[1, b - BEGUN] = imag

    row_is_col = lax.axis_index("row") == lax.axis_index("col")
    multiply = products_of(buf, lhs, jnp.where(row_is_col, 0, 2), put)
    for t in range(NT - TAIL, NT):
        multiply(jnp.int32(t))
    for c in range(2):
        copy = pltpu.make_async_copy(
            last.at[c], out_hbm.at[c, pl.ds(BEGUN, 32 - BEGUN)], sems.at[c, PARTS]
        )
        copy.start()
        copies.append(copy)
    for copy in copies:
        copy.wait()


def hbm(array):
    return pltpu.with_memory_space_constraint(array, pltpu.HBM)


def shards(traces, window_mask):
    dft = jnp.asarray(dft_table().astype(jnp.bfloat16))
    dma = pltpu.SemaphoreType.DMA
    bf16 = jnp.bfloat16
    begun, spectra = pl.pallas_call(
        kernel,
        out_shape=[
            jax.ShapeDtypeStruct((2, BEGUN, 320, 320), bf16),
            jax.ShapeDtypeStruct((NT, 5, 2, 2, 4, NS, LANES), bf16),
        ],
        in_specs=[pl.BlockSpec(memory_space=pltpu.HBM)] * 3,
        out_specs=[pl.BlockSpec(memory_space=pltpu.VMEM)] * 2,
        scratch_shapes=[
            pltpu.VMEM((NT, 6, NS, LANES), bf16),
            pltpu.VMEM((NT, 4, NS, LANES), bf16),
            dma((CHUNKS + 2,)), dma((19,)), dma((RING, 13)),
        ],
        compiler_params=pltpu.CompilerParams(
            collective_id=0, has_side_effects=True, vmem_limit_bytes=14 * 2**20
        ),
        cost_estimate=pl.CostEstimate(
            flops=12 * 10**9, bytes_accessed=20 * 10**6, transcendentals=0
        ),
        name="cross_spectra",
    )(hbm(dft), hbm(jnp.transpose(traces, (1, 0, 2))), hbm(jnp.transpose(window_mask)))
    ended = 32 - BEGUN
    return pl.pallas_call(
        finish_kernel,
        out_shape=jax.ShapeDtypeStruct((2, 32, 320, 320), bf16),
        in_specs=[pl.BlockSpec(memory_space=pltpu.VMEM)] * 2,
        out_specs=pl.BlockSpec(memory_space=pltpu.HBM),
        scratch_shapes=[
            pltpu.VMEM((8 * NS, 4 * LANES), bf16),
            pltpu.VMEM((2, ended, 320, 320), bf16),
            dma((2, PARTS + 1)),
        ],
        compiler_params=pltpu.CompilerParams(vmem_limit_bytes=12 * 2**20),
        name="finish",
    )(begun, spectra)


def solution(mesh):
    placed = (P(("row", "col"), "freq", None), P(("row", "col"), "freq"))
    return jax.shard_map(
        shards, mesh=mesh, in_specs=placed, out_specs=P(None, "freq", "row", "col"), check_vma=False
    )
```

```python
import functools
import math

import jax
import jax.numpy as jnp
import numpy as np
from jax import lax
from jax.experimental import pallas as pl
from jax.experimental.pallas import tpu as pltpu
from jax.sharding import PartitionSpec as P

SAMPLES = 512
BINS = 256
EPSILON = 1e-06
NS = 80
NW = 28
LANES = 128
NT = 14
PERIOD = 7
TAIL = 2
BEGUN = LANES * (NT - TAIL) // (2 * NW)
PARTS = 3
RING = 8
CHUNKS = 2
WINDOWS = 224
MESH = pl.DeviceIdType.MESH
NT_DIMS = (((1,), (1,)), ((), ()))

ORDER = (
    ("T", "own_t", 0),
    ("S", "next_outer", 2),
    ("S", "whole_s", 3),
    ("T", "relay_4", 1),
    ("T", "near_t", 1),
    ("B", "products", 6),
    ("T", "relay_1", 2),
    ("T", "loop_1", 3),
    ("B", "turn", -3),
    ("T", "loop_4", 2),
    ("S", "near_s", 2),
    ("T", "twin_a_t", 1),
    ("T", "whole_t", 3),
    ("T", "relay_2", 3),
    ("S", "own_s", 0),
    ("S", "twin_a_s", 1),
    ("S", "next_far", 3),
    ("T", "rows_t", 4),
    ("S", "rows_s", 4),
)
Z, X1, CA, CB, CL, CR, O4, O1, O2, P4, P1, P2, XW = range(13)


def dft_table():
    t = np.arange(SAMPLES, dtype=np.int64)
    k = np.arange(BINS, dtype=np.int64)
    angles = 2.0 * math.pi / SAMPLES * ((k[:, None] * t[None, :]) % SAMPLES)
    taper = 0.5 - 0.5 * np.cos(2.0 * math.pi / SAMPLES * t)
    stacked = np.stack([taper * np.cos(angles), -taper * np.sin(angles)], axis=1)
    return stacked.reshape(2 * BINS, SAMPLES).astype(np.float32)


def products_of(buf, lhs, r_slot, put):
    lane = lax.broadcasted_iota(jnp.int32, (1, LANES), 1)
    scale = 1.0 / math.sqrt(WINDOWS)

    def rows_of(t, slot, src):
        parts = [buf[t, slot + c % 2, c // 2, src // 4, src % 4] for c in range(4)]
        return jnp.concatenate(parts, axis=0)

    def fold(t, slot, pair, lo, split):
        tiles = []
        for src in (2 * pair, 2 * pair + 1):
            tile = rows_of(t, slot, src)
            if split:
                tile = jnp.where(lane >= lo + LANES, rows_of(t - 1, slot, src), tile)
            tiles.append(tile)
        return jnp.where(place(lo) < LANES // 2, tiles[0], pltpu.roll(tiles[1], LANES // 2, 1))

    def place(lo):
        return (lane - lo + LANES) % LANES

    def one_bin(t, b, split):
        lo = 2 * NW * b - LANES * t
        half = place(lo) % (LANES // 2)
        for pair in range(4):
            tile = fold(t, 0, pair, lo, split)
            ahead = pltpu.roll(tile, LANES - NW, 1)
            back = pltpu.roll(tile, NW, 1)
            turned = jnp.where(half < NW, ahead, -back)
            zero = jnp.zeros_like(tile)
            part = pl.ds(pair * LANES, LANES)
            lhs[pl.ds(0, 4 * NS), part] = jnp.where(half < 2 * NW, tile, zero)
            lhs[pl.ds(4 * NS, 4 * NS), part] = jnp.where(half < 2 * NW, turned, zero)
        rhs = jnp.concatenate([fold(t, r_slot, pair, lo, split) for pair in range(4)], axis=1)
        product = lax.dot_general(
            lhs[...], rhs, NT_DIMS, preferred_element_type=jnp.float32
        )
        product = (product * scale).astype(jnp.bfloat16)
        put(b, product[: 4 * NS], product[4 * NS :])

    def multiply(t):
        first = (LANES * t) // (2 * NW)
        last = (LANES * (t + 1)) // (2 * NW)
        split = (t % PERIOD != 0).astype(jnp.int32)

        @pl.when(t % PERIOD != 0)
        def _():
            one_bin(t, first, True)

        def one(b, carry):
            one_bin(t, b, False)
            return carry

        lax.fori_loop(first + split, last, one, 0)

    return multiply


def kernel(
    dft_hbm, traces_hbm, mask_hbm, out_ref, buf, mine, wbuf, inputs, sends, recvs,
):
    y = lax.axis_index("row")
    col = lax.axis_index("col")
    freq = lax.axis_index("freq")
    xl, core = col // 2, col % 2
    z, xh = freq // 2, freq % 2
    pair_y = y + 1 - 2 * (y % 2)
    outer_y = 3 - y
    far_y = 3 - pair_y
    is_source = (y // 2) == xl
    is_relay = jnp.logical_not(is_source)
    other_col = col + 1 - 2 * core
    x_col = (1 - xl) * 2 + core
    x_freq = z * 2 + 1 - xh

    others = [((z + k) % 4) for k in (1, 3, 2)]
    z_devs = [(y, col, o * 2 + xh) for o in others]
    twin = (y, x_col, freq)
    cross = (y, x_col, x_freq)
    pair = (pair_y, col, freq)
    outer = (outer_y, col, freq)
    mate = (y, other_col, freq)

    barrier = pltpu.get_barrier_semaphore()
    peers = z_devs + [twin, cross, pair, outer, mate]

    def remote(src, dst, send, recv, peer):
        return pltpu.make_async_remote_copy(
            src_ref=src, dst_ref=dst, send_sem=send, recv_sem=recv,
            device_id=peer, device_id_type=MESH,
        )

    def slot_of(row_, col_=col):
        return jnp.where(row_ == col_, 2 + core, 4)

    def free(t, row_, i):
        return buf.at[t, jnp.where(row_ == col, 2, 4), 0, i]

    def piece(t, slot, k):
        a, b = {1: (1 - xl, xh), 2: (xl, 1 - xh), 3: (1 - xl, 1 - xh), 4: (xl, xh)}[k]
        return buf.at[t, slot, a, b]

    def send(t, index, src, dst, recv, peer):
        return remote(src, dst, sends.at[index], recvs.at[t % RING, recv], peer).start()

    def z_sends(t):
        for j in range(6):
            dst = wbuf.at[t, z] if j % 2 else buf.at[t, core, xl, xh, z]
            send(t, j, mine.at[t, j], dst, Z, z_devs[j // 2])

    needs_r = jnp.logical_not(col == y)
    gives_r = jnp.logical_not(other_col == y)

    def same(t, index, place, recv, peer):
        send(t, index, place, place, recv, peer)

    def transform(rows, dft_ref, traces_ref, mask_ref):
        per = NW // CHUNKS
        table = pltpu.make_async_copy(dft_hbm, dft_ref, inputs.at[CHUNKS])
        masks = pltpu.make_async_copy(mask_hbm, mask_ref, inputs.at[CHUNKS + 1])

        def chunk(i):
            part = pl.ds(i * per, per)
            return pltpu.make_async_copy(traces_hbm.at[part], traces_ref.at[part], inputs.at[i])

        table.start()
        masks.start()
        for i in range(CHUNKS):
            chunk(i).start()
        for peer in peers:
            pl.semaphore_signal(barrier, inc=1, device_id=peer, device_id_type=MESH)

        def whiten(w, spectrum):
            energy = jnp.sum(spectrum * spectrum, axis=0, keepdims=True) * (1.0 / SAMPLES)
            factor = mask_ref[pl.ds(w, 1), :].astype(jnp.float32) * lax.rsqrt(energy + EPSILON)
            rows[pl.ds(w, 2 * BINS, stride=NW), :] = spectrum * factor

        def one_chunk(i, carry):
            chunk(i).wait()
            for j in range(per // 2):
                w = i * per + 2 * j
                one, two = traces_ref[w], traces_ref[w + 1]
                spare = LANES - NS
                both = jnp.concatenate([one, two[:spare], two, one[:spare]], axis=0)
                spectrum = lax.dot_general(
                    dft_ref[...], both, NT_DIMS, preferred_element_type=jnp.float32
                )
                whiten(w, spectrum[:, :NS])
                whiten(w + 1, spectrum[:, LANES : LANES + NS])
            return carry

        table.wait()
        masks.wait()
        lax.fori_loop(0, CHUNKS, one_chunk, 0)
        pl.semaphore_wait(barrier, len(peers))

    def wait_only(ref, sem):
        pltpu.make_async_copy(ref, ref, sem).wait()

    def main(rows, lhs):
        def turn(t):
            for k in range(4):
                for i in range(2):
                    f = ((z + (0, 1, 3, 2)[k]) % 4) * 2 + (1 - xh if i else xh)
                    start = pl.multiple_of((f * NT + t) * LANES, LANES)
                    turned = rows[pl.ds(start, LANES), :].T.astype(jnp.bfloat16)
                    if k:
                        mine[t, 2 * (k - 1) + i] = turned
                    elif i:
                        wbuf[t, z] = turned
                    else:
                        buf[t, core, xl, xh, z] = turned
            z_sends(t)

        def put(b, real, imag):
            out_ref[0, b] = real
            out_ref[1, b] = imag

        multiply = products_of(buf, lhs, jnp.where(col == y, 0, 2), put)

        def own(t):
            wait_only(mine.at[t], recvs.at[t % RING, Z])
            send(t, 6, wbuf.at[t], piece(t, core, 4), X1, cross)
            same(t, 7, piece(t, core, 4), CA, twin)

        def own_s(t):
            own(t)
            send(t, 11, piece(t, core, 4), piece(t, slot_of(y), 4), O4, outer)

        def own_t(t):
            own(t)
            send(t, 11, wbuf.at[t], free(t, outer_y, 0), O4, outer)

        def near(t):
            wait_only(piece(t, core, 3), recvs.at[t % RING, X1])
            same(t, 8, piece(t, core, 3), CB, twin)

        def near_s(t):
            near(t)
            send(t, 12, piece(t, core, 3), piece(t, slot_of(y), 3), P2, pair)

        def twin_a(t):
            wait_only(piece(t, core, 1), recvs.at[t % RING, CA])

        def twin_a_s(t):
            twin_a(t)
            send(t, 13, piece(t, core, 1), piece(t, slot_of(y), 1), O1, outer)

        def whole(t):
            wait_only(piece(t, core, 2), recvs.at[t % RING, CB])

        def whole_s(t):
            whole(t)
            send(t, 15, piece(t, core, 2), piece(t, slot_of(y), 2), O2, outer)
            send(t, 14, piece(t, core, 2), piece(t, slot_of(y), 2), P2, pair)
            same(t, 9, buf.at[t, core], CL, mate)

        def whole_t(t):
            whole(t)
            same(t, 9, buf.at[t, core], CL, mate)

        def relay(t, index, k, recv, recv_next):
            held = piece(t, slot_of(outer_y), k)
            wait_only(held, recvs.at[t % RING, recv])
            same(t, index, held, recv_next, pair)

        def relay_4(t):
            relay(t, 12, 4, O4, P4)

        def relay_1(t):
            relay(t, 13, 1, O1, P1)

        def relay_2(t):
            relay(t, 14, 2, O2, P2)

        def next_outer(t):
            held = free(t, y, 0)
            wait_only(held, recvs.at[t % RING, O4])
            send(t, 16, held, free(t, pair_y, 1), P4, pair)
            send(t, 17, held, buf.at[t, slot_of(outer_y, x_col), xl, xh], XW, cross)

        def next_far(t):
            held = free(t, y, 1)
            wait_only(held, recvs.at[t % RING, P4])
            send(t, 18, held, buf.at[t, slot_of(far_y, x_col), xl, xh], XW, cross)

        def loop(t, index, k, recv):
            held = piece(t, slot_of(far_y), k)
            wait_only(held, recvs.at[t % RING, recv])
            same(t, index, held, O1, outer)

        def loop_4(t):
            loop(t, 15, 4, P4)

        def loop_1(t):
            loop(t, 16, 1, P1)

        def give(t):
            @pl.when(gives_r)
            def _():
                send(t, 10, buf.at[t, 4], buf.at[t, 2 + core], CR, mate)

        def rows_s(t):
            wait_only(buf.at[t, 4, xl], recvs.at[t % RING, P2])
            wait_only(buf.at[t, 4, xl], recvs.at[t % RING, O1])
            give(t)

        def rows_t(t):
            wait_only(piece(t, slot_of(far_y), 2), recvs.at[t % RING, P2])
            wait_only(buf.at[t, 4, xl], recvs.at[t % RING, XW])
            give(t)

        def products(t):
            wait_only(buf.at[t, 1 - core], recvs.at[t % RING, CL])

            @pl.when(needs_r)
            def _():
                wait_only(buf.at[t, 3 - core], recvs.at[t % RING, CR])

            @pl.when(t < NT - TAIL)
            def _():
                multiply(t)

        events = {
            "turn": turn, "products": products,
            "own_s": own_s, "near_s": near_s, "twin_a_s": twin_a_s, "whole_s": whole_s,
            "next_outer": next_outer, "next_far": next_far, "rows_s": rows_s,
            "own_t": own_t, "near_t": near, "twin_a_t": twin_a, "whole_t": whole_t,
            "relay_4": relay_4, "relay_1": relay_1, "relay_2": relay_2,
            "loop_4": loop_4, "loop_1": loop_1, "rows_t": rows_t,
        }

        def step(tau, carry):
            for who, name, lag in ORDER:
                run = jnp.logical_and(tau >= lag, tau < NT + lag)
                if who != "B":
                    run = jnp.logical_and(run, is_source if who == "S" else is_relay)

                @pl.when(run)
                def _():
                    events[name](tau - lag)

            return carry

        lags = {name: lag for _, name, lag in ORDER}
        for t in range(-lags["turn"]):
            turn(t)
        lax.fori_loop(0, NT + max(lags.values()), step, 0)

    def stages(rows):
        pl.run_scoped(
            functools.partial(transform, rows),
            pltpu.VMEM((2 * BINS, SAMPLES), jnp.bfloat16),
            pltpu.VMEM((NW, NS, SAMPLES), jnp.bfloat16),
            pltpu.VMEM((NW, NS), jnp.int32),
        )
        pl.run_scoped(
            lambda lhs: main(rows, lhs), pltpu.VMEM((8 * NS, 4 * LANES), jnp.bfloat16)
        )

    pl.run_scoped(stages, pltpu.VMEM((2 * BINS * NW, NS), jnp.float32))

    one, two = wbuf, buf.at[:, core]
    for j in range(6):
        wait_only(mine.at[:, j], sends.at[j])
    for j in (6, 7, 8, 11, 12, 13, 14, 15, 16):
        wait_only(one, sends.at[j])
    wait_only(two, sends.at[9])

    @pl.when(gives_r)
    def _():
        wait_only(two, sends.at[10])

    @pl.when(is_source)
    def _():
        for j in (17, 18):
            wait_only(one, sends.at[j])


def finish_kernel(begun, buf, out_hbm, lhs, last, sems):
    per = BEGUN // PARTS
    copies = []
    for c in range(2):
        for i in range(PARTS):
            part = pl.ds(i * per, per)
            copies.append(
                pltpu.make_async_copy(begun.at[c, part], out_hbm.at[c, part], sems.at[c, i])
            )
    for copy in copies:
        copy.start()

    def put(b, real, imag):
        last[0, b - BEGUN] = real
        last[1, b - BEGUN] = imag

    row_is_col = lax.axis_index("row") == lax.axis_index("col")
    multiply = products_of(buf, lhs, jnp.where(row_is_col, 0, 2), put)
    for t in range(NT - TAIL, NT):
        multiply(jnp.int32(t))
    for c in range(2):
        copy = pltpu.make_async_copy(
            last.at[c], out_hbm.at[c, pl.ds(BEGUN, 32 - BEGUN)], sems.at[c, PARTS]
        )
        copy.start()
        copies.append(copy)
    for copy in copies:
        copy.wait()


def hbm(array):
    return pltpu.with_memory_space_constraint(array, pltpu.HBM)


def shards(traces, window_mask):
    dft = jnp.asarray(dft_table().astype(jnp.bfloat16))
    dma = pltpu.SemaphoreType.DMA
    bf16 = jnp.bfloat16
    begun, spectra = pl.pallas_call(
        kernel,
        out_shape=[
            jax.ShapeDtypeStruct((2, BEGUN, 320, 320), bf16),
            jax.ShapeDtypeStruct((NT, 5, 2, 2, 4, NS, LANES), bf16),
        ],
        in_specs=[pl.BlockSpec(memory_space=pltpu.HBM)] * 3,
        out_specs=[pl.BlockSpec(memory_space=pltpu.VMEM)] * 2,
        scratch_shapes=[
            pltpu.VMEM((NT, 6, NS, LANES), bf16),
            pltpu.VMEM((NT, 4, NS, LANES), bf16),
            dma((CHUNKS + 2,)), dma((19,)), dma((RING, 13)),
        ],
        compiler_params=pltpu.CompilerParams(
            collective_id=0, has_side_effects=True, vmem_limit_bytes=14 * 2**20
        ),
        cost_estimate=pl.CostEstimate(
            flops=12 * 10**9, bytes_accessed=20 * 10**6, transcendentals=0
        ),
        name="cross_spectra",
    )(hbm(dft), hbm(jnp.transpose(traces, (1, 0, 2))), hbm(jnp.transpose(window_mask)))
    ended = 32 - BEGUN
    return pl.pallas_call(
        finish_kernel,
        out_shape=jax.ShapeDtypeStruct((2, 32, 320, 320), bf16),
        in_specs=[pl.BlockSpec(memory_space=pltpu.VMEM)] * 2,
        out_specs=pl.BlockSpec(memory_space=pltpu.HBM),
        scratch_shapes=[
            pltpu.VMEM((8 * NS, 4 * LANES), bf16),
            pltpu.VMEM((2, ended, 320, 320), bf16),
            dma((2, PARTS + 1)),
        ],
        compiler_params=pltpu.CompilerParams(vmem_limit_bytes=12 * 2**20),
        name="finish",
    )(begun, spectra)


def solution(mesh):
    placed = (P(("row", "col"), "freq", None), P(("row", "col"), "freq"))
    return jax.shard_map(
        shards, mesh=mesh, in_specs=placed, out_specs=P(None, "freq", "row", "col"), check_vma=False
    )
```
